32 devices in a mesh: group: 4 (over z), dev: 8 (over y, x, core).
Axes of the slice: x: 2, y: 2, z: 4, core: 2. Of those that a mesh axis runs over, the one named last changes fastest.
Arguments:
- expert_input: bfloat16 [2, 192, 4096], P(None, ('group', 'dev')), may hold values from -6 to 6
- expert_ids: int32 [2, 192, 2], P(None, ('group', 'dev')), may hold values from 0 to 3, all different within a row; in each aligned block of 6 rows (0 to 5, 6 to 11, ..., all dimensions but the last counted through in order) at most 3 rows name the same one
- combine: float32 [2, 192, 2], P(None, ('group', 'dev')), may hold values from 0.25 to 1
- gate_weight: bfloat16 [8, 4096, 6144], P('dev', None, 'group'), may hold values from -0.09375 to 0.09375
- up_weight: bfloat16 [8, 4096, 6144], P('dev', None, 'group'), may hold values from -0.09375 to 0.09375
- down_weight: bfloat16 [8, 6144, 4096], P('dev', 'group'), may hold values from -0.0546875 to 0.0546875
Outputs:
- moe_out: bfloat16 [2, 192, 4096], P(None, ('group', 'dev'))
The draws below stay inside these ranges and needn't reach their ends.
Inputs may be any that keep to these rules, and one draw needn't show every extreme that they name: `expert_ids`: the two experts of a row differ; among the rows of one device in one step no expert is named more than 3 times.
All inputs are finite; a program needn't handle non-finite values.
Results may differ from the reference program's by a relative error of at most 0.017.
Values may be sent and summed in bfloat16 or wider, within the bound.
No kernel may reach another device: no remote copies, remote signals or barrier semaphores. Data moves between devices by JAX's collectives and lax.ppermute only.
A program may use at most 128 MiB of HBM per device.

```python
import math
import jax
import jax.numpy as jnp
import numpy as np
from jax import lax

D = 4096
FF = 12288
STEPS = 2
ROWS_DEV = 6
EXPERTS = 4
SLOT = 3
FF_DEV = 1536
ROWS = 192
N_GROUP = 4
N_DEV = 8


def shard_levels(rng, extent, split, least, top_value):
    def one(dim, shards_of):
        heights = jax.random.uniform(jax.random.fold_in(jax.random.fold_in(rng, 6), dim), (shards_of,), jnp.float32, least / len(split), top_value / len(split))
        return jnp.repeat(jnp.exp(heights), extent[dim] // shards_of).reshape((-1,) + (1,) * (len(extent) - dim - 1))

    loudness = one(*split[0])
    for cut in split[1:]:
        loudness = loudness * one(*cut)
    return loudness


def assign_block(key, own, number, rows, amount, top, reach, lean):
    ranking = jax.random.permutation(key, amount)
    heavy_load, ordinary = portions_of(amount, rows * top, reach, lean, True), portions_of(amount, rows * top, reach, lean, False)
    places = jnp.arange(amount)

    def named(lengths, turn):
        used = int((lengths > 0).sum())
        fixed = max(1, used // 4)
        shifted = fixed + (places - fixed + turn * (used - fixed)) % max(1, amount - fixed)
        return jnp.zeros((amount,), jnp.int32).at[ranking[jnp.where(places < fixed, places, shifted)]].set(jnp.asarray(lengths, jnp.int32))

    lengths = jnp.where(number % 4 == 0, named(heavy_load, number // 4), named(ordinary, number - number // 4 - 1))
    mixed = jax.random.permutation(jax.random.fold_in(own, 3), amount)
    source_of, receiver = mixed[0:amount // 2 * 2:2], mixed[1:amount // 2 * 2:2]
    margin = jnp.minimum(lengths[source_of] - 1, reach - lengths[receiver]) // 2
    margin = jnp.where((source_of == ranking[0]) | (receiver == ranking[0]) | (lengths[receiver] == 0), 0, jnp.maximum(margin, 0))
    shifted = jax.random.randint(jax.random.fold_in(own, 4), (amount // 2,), 0, 1 << 20) % (margin + 1)
    lengths = lengths.at[source_of].add(-shifted).at[receiver].add(shifted)
    members = jnp.searchsorted(jnp.cumsum(lengths), jnp.arange(rows * top), side="right").astype(jnp.int32)
    grid = members.reshape(top, rows).T
    grid = grid[jax.random.permutation(jax.random.fold_in(own, 1), rows)]
    turn = jax.random.randint(jax.random.fold_in(own, 2), (rows, 1), 0, top)
    return jnp.take_along_axis(grid, (jnp.arange(top)[None, :] + turn) % top, axis=1)


def portions_of(number_of, total, reach, skew, full):
    portions = [(1 << 20) // math.isqrt(grade ** skew) + 1 for grade in range(1, number_of + 1)]
    largest = reach if full else min(reach, max(-(-total // number_of), total * portions[0] // sum(portions)))
    least = 1 if total - largest >= number_of - 1 else 0
    given, surplus = [largest] + [least] * (number_of - 1), total - largest - least * (number_of - 1)
    while surplus > 0:
        candidates = [i for i in range(1, number_of) if given[i] < largest] or [i for i in range(1, number_of) if given[i] < reach]
        whole, budget = sum([portions[i] for i in candidates]), surplus
        for i in candidates:
            extra = min(reach - given[i], max(1, budget * portions[i] // whole), surplus)
            given[i] = given[i] + extra
            surplus = surplus - extra
    return np.array(given)


def gaussian(stream_key, extent, scale, most, pieces=(), held_as=jnp.bfloat16):
    level = shard_levels(stream_key, extent, pieces, -0.22, 0.18) if pieces else 1.0
    array = jax.random.normal(stream_key, extent, jnp.float32) * scale * level
    return jnp.minimum(jnp.maximum(array, -most), most).astype(held_as)


def setup_inputs(seed: int = 0) -> dict:
    splits = jax.random.split(jax.random.key(seed), 7)
    expert_input = gaussian(splits[0], (STEPS, ROWS, D), 1.0, 6.0, ((1, 32),))
    expert_ids_keys = jax.random.split(jax.random.fold_in(splits[1], 1), STEPS * ROWS // ROWS_DEV)
    expert_ids_turns = jax.random.permutation(jax.random.fold_in(splits[1], 3), STEPS * ROWS // ROWS_DEV)
    expert_ids = jax.vmap(lambda own, number: assign_block(jax.random.fold_in(splits[1], 2), own, number, ROWS_DEV, EXPERTS, 2, SLOT, 2))(expert_ids_keys, expert_ids_turns).reshape((STEPS, ROWS, 2))
    combine = jnp.clip(0.25 + 0.75 * jax.random.uniform(splits[2], (STEPS, ROWS, 2), jnp.float32) ** shard_levels(splits[2], (STEPS, ROWS, 2), ((1, 32),), -0.2, 0.2), 0.25, 1.0)
    gate_weight = gaussian(splits[3], (2 * EXPERTS, D, FF // 2), D ** -0.5, 0.09375, ((0, 8), (2, 4)))
    up_weight = gaussian(splits[4], (2 * EXPERTS, D, FF // 2), D ** -0.5, 0.09375, ((0, 8), (2, 4)))
    down_weight = gaussian(splits[5], (2 * EXPERTS, FF // 2, D), FF ** -0.5, 0.0546875, ((0, 8), (1, 4)))
    return dict(expert_input=expert_input, expert_ids=expert_ids, combine=combine, gate_weight=gate_weight, up_weight=up_weight, down_weight=down_weight)


def reference(expert_input, expert_ids, combine, gate_weight, up_weight, down_weight):
    device_total = N_GROUP * N_DEV
    slot_total = device_total * SLOT
    outputs = []
    for moment in range(STEPS):
        chosen_ids = expert_ids[moment].reshape(device_total, 2 * ROWS_DEV)
        named_hits = (chosen_ids[:, :, None] == jnp.arange(EXPERTS, dtype=jnp.int32)[None, None, :]).astype(jnp.int32)
        earlier = jnp.cumsum(named_hits, 1) - named_hits
        position = jnp.sum(earlier * named_hits, 2)
        buffer_index = (jnp.arange(device_total, dtype=jnp.int32)[:, None] * SLOT + position).astype(jnp.int32)
        row_index = jnp.arange(device_total, dtype=jnp.int32)[:, None] * ROWS_DEV + jnp.arange(2 * ROWS_DEV, dtype=jnp.int32)[None, :] // 2
        table = jnp.zeros((EXPERTS, slot_total), jnp.int32).at[chosen_ids.reshape(-1), buffer_index.reshape(-1)].set(row_index.reshape(-1).astype(jnp.int32))
        filled = jnp.zeros((EXPERTS, slot_total), jnp.float32).at[chosen_ids.reshape(-1), buffer_index.reshape(-1)].set(1.0)
        tokens = expert_input[moment]

        def one_expert(expert):
            picked_rows = jnp.take(tokens, table[expert], axis=0) * filled[expert][:, None].astype(jnp.bfloat16)
            value = jnp.zeros((slot_total, D), jnp.float32)
            for half_index in range(2):
                entry = 2 * expert + half_index
                gate_half = lax.dynamic_index_in_dim(gate_weight, entry, 0, keepdims=False)
                up_half = lax.dynamic_index_in_dim(up_weight, entry, 0, keepdims=False)
                down_half = lax.dynamic_index_in_dim(down_weight, entry, 0, keepdims=False)
                gate_val = jnp.dot(picked_rows, gate_half, preferred_element_type=jnp.float32)
                up_val = jnp.dot(picked_rows, up_half, preferred_element_type=jnp.float32)
                hidden = (jax.nn.silu(gate_val) * up_val).astype(jnp.bfloat16)
                blocks = hidden.reshape(slot_total, N_GROUP, FF_DEV).astype(jnp.float32)
                down_blocks = down_half.reshape(N_GROUP, FF_DEV, D).astype(jnp.float32)
                product = jnp.einsum("sgf,gfx->gsx", blocks, down_blocks).astype(jnp.bfloat16)
                half_sum = jnp.sum(product.astype(jnp.float32), 0).astype(jnp.bfloat16)
                value = value + half_sum.astype(jnp.float32)
            return value

        values = lax.map(one_expert, jnp.arange(EXPERTS, dtype=jnp.int32))
        picked = values[expert_ids[moment], buffer_index.reshape(ROWS, 2)]
        outputs.append(jnp.sum(combine[moment][:, :, None] * picked, 1).astype(jnp.bfloat16))
    return jnp.stack(outputs, 0)
```

```python
import functools

import jax
import jax.numpy as jnp
from jax import lax
from jax.experimental import pallas as pl
from jax.experimental.pallas import tpu as pltpu
from jax.sharding import PartitionSpec as P

BF = jnp.bfloat16
F32 = jnp.float32
LANES = 128
SUB = 8
FOLD = 16


def whole(memory_space=pltpu.VMEM):
    return pl.BlockSpec(memory_space=memory_space)


def call(body, outs, args, name, spaces=None, scratch=(), limit=12):
    spaces = spaces or [pltpu.VMEM] * len(args)
    return pl.pallas_call(
        body,
        out_shape=[jax.ShapeDtypeStruct(s, BF) for s in outs],
        in_specs=[whole(s) for s in spaces],
        out_specs=[whole() for _ in outs],
        scratch_shapes=list(scratch),
        name=name,
        compiler_params=pltpu.CompilerParams(vmem_limit_bytes=limit << 20),
    )(*args)


def pack_body(experts, slots, ids_ref, combine_ref, x_ref, o_ref):
    steps, rows, width = x_ref.shape
    half = width // 2
    own = lax.axis_index("dev") // 2
    table_rows = experts * steps * slots
    row_at = lax.broadcasted_iota(jnp.int32, (table_rows, LANES), 0)
    lane = lax.broadcasted_iota(jnp.int32, (table_rows, LANES), 1)
    group, place = lane // FOLD, lane % FOLD
    low = jnp.where((group == 1) & (place >= 12), place - 4, jnp.where((group == 1) & (place >= SUB), -1, place))
    table = jnp.zeros((table_rows, LANES), F32)
    for t in range(steps):
        counts = [jnp.int32(0)] * experts
        for r in range(rows):
            for k in range(2):
                e = ids_ref[t, r, k]
                position = jnp.int32(0)
                for c in range(experts):
                    position = jnp.where(e == c, counts[c], position)
                counts = [counts[c] + (e == c).astype(jnp.int32) for c in range(experts)]
                slot = ((e ^ own) * steps + t) * slots + position
                hit = (row_at == slot) & (low == t * rows + r)
                table = jnp.where(hit, combine_ref[t, r, k], table)
    ones = jnp.where(table != 0.0, 1.0, 0.0)
    high = table.astype(BF).astype(F32)
    middle = (table - high).astype(BF).astype(F32)
    rest = table - high - middle
    coded = jnp.where(
        group <= 1, ones, jnp.where(group == 2, high, jnp.where(group == 3, middle, jnp.where(group == 4, rest, 0.0)))
    ).astype(BF)
    flat = jnp.concatenate([x_ref[t].astype(F32) for t in range(steps)], 0)
    tail = flat[SUB:]
    o_ref[:, :width] = flat[:SUB].astype(BF)
    o_ref[:, width : width + half] = jnp.concatenate([tail[:, :half], tail[:, half:]], 0).astype(BF)
    for b in range(table_rows // SUB):
        start = width + half + b * LANES
        o_ref[:, start : start + LANES] = coded[b * SUB : (b + 1) * SUB]


def tables_of(packed, experts, pair, width, group):
    base = width + width // 2
    members = len(packed)
    table_rows = experts * pair
    total = table_rows * members
    blocks = []
    for k, ref in enumerate(packed):
        tab = jnp.concatenate(
            [ref[:, base + b * LANES : base + (b + 1) * LANES] for b in range(table_rows // SUB)], 0
        ).astype(F32)
        at = k % (LANES // FOLD)
        shift = (at - group) * FOLD % LANES
        moved = pltpu.roll(tab, shift, 1) if shift else tab
        lane = lax.broadcasted_iota(jnp.int32, moved.shape, 1)
        moved = jnp.where(lane // FOLD == at, moved, 0.0)
        tiles = [jnp.zeros_like(moved)] * -(-members * FOLD // LANES)
        tiles[k * FOLD // LANES] = moved
        blocks.append(jnp.concatenate(tiles, 1))
    stacked = jnp.concatenate(blocks, 0).astype(BF)
    to = lax.broadcasted_iota(jnp.int32, (total, total), 0)
    source = lax.broadcasted_iota(jnp.int32, (total, total), 1)
    e, k, p = to // (members * pair), to // pair % members, to % pair
    order = jnp.where(source == k * table_rows + e * pair + p, 1.0, 0.0).astype(BF)
    return jnp.dot(order, stacked, preferred_element_type=F32).astype(BF)[:, : members * FOLD]


def route_body(experts, pair, width, *refs):
    members = len(refs) - experts
    packed, outs = refs[:members], refs[members:]
    half = width // 2
    block = members * pair
    for side in range(2):
        pick = tables_of(packed, experts, pair, width, side)
        rows = jnp.concatenate(
            [part for ref in packed for part in (ref[:, side * half : (side + 1) * half], ref[:, width : width + half])], 0
        )
        got = jnp.dot(pick, rows, preferred_element_type=F32).astype(BF)
        for j in range(experts):
            outs[j][:, side * half : (side + 1) * half] = got[j * block : (j + 1) * block]


def up_body(count, *refs):
    blocks, gate_ref, up_ref, hidden_ref, rows_ref = refs[:count], refs[count], refs[count + 1], refs[count + 2], refs[count + 3]
    rows = jnp.concatenate([b[...] for b in blocks], 0)
    rows_ref[...] = rows
    tile = 256

    def step(j, carry):
        columns = pl.ds(pl.multiple_of(j * tile, tile), tile)
        gate = jnp.dot(rows_ref[...], gate_ref[:, columns], preferred_element_type=F32)
        up = jnp.dot(rows_ref[...], up_ref[:, columns], preferred_element_type=F32)
        hidden_ref[:, columns] = (jax.nn.silu(gate) * up).astype(BF)
        return carry

    lax.fori_loop(0, hidden_ref.shape[1] // tile, step, 0)


def down_body(hidden_ref, down_ref, own_ref, other_ref):
    tile = 512
    mine = own_ref.shape[0]

    def step(j, carry):
        columns = pl.ds(pl.multiple_of(j * tile, tile), tile)
        value = jnp.dot(hidden_ref[...], down_ref[:, columns], preferred_element_type=F32).astype(BF)
        own_ref[:, columns] = value[:mine]
        other_ref[:, columns] = value[mine:]
        return carry

    lax.fori_loop(0, own_ref.shape[1] // tile, step, 0)


def add_body(own_ref, got_ref, *outs):
    block = outs[0].shape[0]
    for j, out in enumerate(outs):
        at = slice(j * block, (j + 1) * block)
        out[...] = (own_ref[at].astype(F32) + got_ref[at].astype(F32)).astype(BF)


def blend_body(experts, pair, width, members, *refs):
    packed, values, outs = refs[:members], refs[members : members + experts], refs[members + experts :]
    half = width // 2
    parts = [tables_of(packed, experts, pair, width, g) for g in (2, 3, 4)]
    weights = jnp.concatenate(parts, 1)
    span = members * FOLD
    tails = []
    for side in range(2):
        cols = slice(side * half, (side + 1) * half)
        value = jnp.concatenate([v[:, cols] for v in values], 0)
        total = lax.dot_general(weights, value, (((0,), (0,)), ((), ())), preferred_element_type=F32)
        total = total[:span] + total[span : 2 * span] + total[2 * span :]
        for k, out in enumerate(outs):
            out[:, cols] = total[k * FOLD : k * FOLD + SUB].astype(BF)
        tails.append([total[k * FOLD + SUB : k * FOLD + SUB + 4] for k in range(members)])
    for k, out in enumerate(outs):
        out[:, width : width + half] = jnp.concatenate([tails[0][k], tails[1][k]], 0).astype(BF)


def finish_body(*refs):
    parts, out_ref = refs[:-1], refs[-1]
    steps, rows, width = out_ref.shape
    half = width // 2
    total = parts[0][...].astype(F32)
    for p in parts[1:]:
        total = total + p[...].astype(F32)
    tail = total[:, width : width + half]
    tail = jnp.concatenate([tail[:4], tail[4:]], 1)
    flat = jnp.concatenate([total[:, :width], tail], 0)
    for t in range(steps):
        out_ref[t] = flat[t * rows : (t + 1) * rows].astype(BF)


def local(expert_input, expert_ids, combine, gate_weight, up_weight, down_weight):
    members = lax.axis_size("group")
    devices = lax.axis_size("dev")
    experts = devices // 2
    steps, row_count, width = expert_input.shape
    slots = max(2, (2 * row_count + experts - 1) // experts)
    pair = steps * slots
    packed_width = width + width // 2 + experts * pair // SUB * LANES
    block = members * pair

    (packed,) = call(
        functools.partial(pack_body, experts, slots),
        [(SUB, packed_width)],
        (expert_ids, combine, expert_input),
        "pack",
        [pltpu.SMEM, pltpu.SMEM, pltpu.VMEM],
    )
    far = sorted(range(1, members), key=lambda k: -min(k, members - k))
    gathered = {0: packed}
    for k in far:
        gathered[k] = lax.ppermute(packed, "group", [(i, (i + k) % members) for i in range(members)])
    gathered = [gathered[k] for k in range(members)]

    routed = call(
        functools.partial(route_body, experts, pair, width), [(block, width)] * experts, gathered, "route"
    )

    def exchange(arrays):
        order = sorted(range(1, experts), key=lambda j: -bin(j).count("1"))
        got = {0: arrays[0]}
        for j in order:
            got[j] = lax.ppermute(arrays[j], "dev", [(i, i ^ (2 * j)) for i in range(devices)])
        return [got[j] for j in range(experts)]

    def swap(array):
        return lax.ppermute(array, "dev", [(i, i ^ 1) for i in range(devices)])

    mine = exchange(routed)
    theirs = [swap(a) for a in mine]
    rows_all = 2 * experts * block
    hidden_units = gate_weight.shape[2]
    (hidden,) = call(
        functools.partial(up_body, 2 * experts),
        [(rows_all, hidden_units)],
        (*mine, *theirs, gate_weight[0], up_weight[0]),
        "gate_up",
        scratch=[pltpu.VMEM((rows_all, width), BF)],
    )
    own, other = call(down_body, [(rows_all // 2, width)] * 2, (hidden, down_weight[0]), "down")
    halves = call(add_body, [(block, width)] * experts, (own, swap(other)), "add")
    returned = exchange(halves)
    blended = call(
        functools.partial(blend_body, experts, pair, width, members),
        [(SUB, width + width // 2)] * members,
        (*gathered, *returned),
        "blend",
    )
    final = {0: blended[0]}
    for k in far:
        final[k] = lax.ppermute(blended[k], "group", [(i, (i - k) % members) for i in range(members)])
    (out,) = call(finish_body, [expert_input.shape], [final[k] for k in range(members)], "finish")
    return out


def solution(mesh):
    in_specs = (
        P(None, ("group", "dev"), None),
        P(None, ("group", "dev"), None),
        P(None, ("group", "dev"), None),
        P("dev", None, "group"),
        P("dev", None, "group"),
        P("dev", "group", None),
    )
    out_specs = P(None, ("group", "dev"), None)
    return jax.shard_map(local, mesh=mesh, in_specs=in_specs, out_specs=out_specs, check_vma=False)
```

```python
import functools

import jax
import jax.numpy as jnp
from jax import lax
from jax.experimental import pallas as pl
from jax.experimental.pallas import tpu as pltpu
from jax.sharding import PartitionSpec as P

BF = jnp.bfloat16
F32 = jnp.float32
LANES = 128
SUB = 8
FOLD = 16
UNIT_TILE = 256
PIECES = 8
PARTS = 2


def whole(memory_space=pltpu.VMEM):
    return pl.BlockSpec(memory_space=memory_space)


def pinned(array):
    return pltpu.with_memory_space_constraint(array, pltpu.HBM)


def call(body, outs, args, name, spaces=None, scratch=(), limit=12, flops=0, moved=0):
    spaces = spaces or [pltpu.VMEM] * len(args)
    return pl.pallas_call(
        body,
        out_shape=[jax.ShapeDtypeStruct(s, BF) if isinstance(s, tuple) else s for s in outs],
        in_specs=[whole(s) for s in spaces],
        out_specs=[whole() for _ in outs],
        scratch_shapes=list(scratch),
        name=name,
        compiler_params=pltpu.CompilerParams(vmem_limit_bytes=limit << 20),
        cost_estimate=pl.CostEstimate(flops=flops, bytes_accessed=moved, transcendentals=0),
    )(*args)


def by_core(first, second):
    core = lax.axis_index("dev") % 2
    pl.when(core == 0)(first)
    pl.when(core == 1)(second)


def padded(rows):
    missing = -rows.shape[0] % SUB
    return jnp.concatenate([rows, jnp.zeros((missing, rows.shape[1]), rows.dtype)], 0) if missing else rows


def weigh_rows(weights, value, span):
    total = lax.dot_general(weights, value, (((0,), (0,)), ((), ())), preferred_element_type=F32)
    return total[:span] + total[span : 2 * span] + total[2 * span :]


def pack_body(experts, slots, ids_hbm, combine_hbm, x_hbm, *refs):
    outs, table_out, (ids_ref, combine_ref, x_ref, sems) = refs[:-5], refs[-5], refs[-4:]
    copies = [
        pltpu.make_async_copy(source, target, sems.at[i])
        for i, (source, target) in enumerate(((ids_hbm, ids_ref), (combine_hbm, combine_ref), (x_hbm, x_ref)))
    ]
    for copy in copies:
        copy.start()
    rows, steps, width = x_ref.shape
    half = width // 2
    pair = steps * slots
    own = lax.axis_index("dev") // 2
    table_rows = experts * pair
    row_at = lax.broadcasted_iota(jnp.int32, (table_rows, LANES), 0)
    lane = lax.broadcasted_iota(jnp.int32, (table_rows, LANES), 1)
    group, place = lane // FOLD, lane % FOLD
    low = jnp.where((group == 1) & (place >= 12), place - 4, jnp.where((group == 1) & (place >= SUB), -1, place))
    table = jnp.zeros((table_rows, LANES), F32)
    copies[0].wait()
    copies[1].wait()
    for t in range(steps):
        counts = [jnp.int32(0)] * experts
        for r in range(rows):
            for k in range(2):
                e = ids_ref[t, k, r]
                position = jnp.int32(0)
                for c in range(experts):
                    position = jnp.where(e == c, counts[c], position)
                counts = [counts[c] + (e == c).astype(jnp.int32) for c in range(experts)]
                slot = ((e ^ own) * steps + t) * slots + position
                hit = (row_at == slot) & (low == r * steps + t)
                table = jnp.where(hit, combine_ref[t, k, r], table)
    ones = jnp.where(table != 0.0, 1.0, 0.0)
    high = table.astype(BF).astype(F32)
    middle = (table - high).astype(BF).astype(F32)
    rest = table - high - middle
    coded = jnp.where(
        group <= 1, ones, jnp.where(group == 2, high, jnp.where(group == 3, middle, jnp.where(group == 4, rest, 0.0)))
    ).astype(BF)
    table_out[...] = coded
    copies[2].wait()
    flat = jnp.concatenate([x_ref[r].astype(F32) for r in range(rows)], 0)

    def first():
        tail = flat[SUB:]
        top = flat[:SUB].astype(BF)
        fold = jnp.concatenate([tail[:, :half], tail[:, half:]], 0).astype(BF)
        for out in outs:
            out[:, :width] = top
            out[:, width : width + half] = fold
            for b in range(table_rows // SUB):
                start = width + half + b * LANES
                out[:, start : start + LANES] = coded[b * SUB : (b + 1) * SUB]

    def second():
        source = jnp.concatenate([flat, jnp.zeros((FOLD - flat.shape[0], width), F32)], 0).astype(BF)
        got = jnp.dot(coded[:, :FOLD], source, preferred_element_type=F32)
        for j, out in enumerate(outs):
            if j < experts:
                out[:, :width] = padded(got[j * pair : (j + 1) * pair]).astype(BF)
            else:
                out[:, :width] = jnp.zeros((SUB, width), BF)
            out[:, width:] = jnp.zeros((SUB, out.shape[1] - width), BF)

    by_core(first, second)


def tables_of(packed, experts, pair, width, group):
    base = width + width // 2
    members = len(packed)
    table_rows = experts * pair
    total = table_rows * members
    blocks = []
    for k, ref in enumerate(packed):
        tab = jnp.concatenate(
            [ref[:, base + b * LANES : base + (b + 1) * LANES] for b in range(table_rows // SUB)], 0
        ).astype(F32)
        at = k % (LANES // FOLD)
        shift = (at - group) * FOLD % LANES
        moved = pltpu.roll(tab, shift, 1) if shift else tab
        lane = lax.broadcasted_iota(jnp.int32, moved.shape, 1)
        moved = jnp.where(lane // FOLD == at, moved, 0.0)
        tiles = [jnp.zeros_like(moved)] * -(-members * FOLD // LANES)
        tiles[k * FOLD // LANES] = moved
        blocks.append(jnp.concatenate(tiles, 1))
    stacked = jnp.concatenate(blocks, 0).astype(BF)
    to = lax.broadcasted_iota(jnp.int32, (total, total), 0)
    source = lax.broadcasted_iota(jnp.int32, (total, total), 1)
    e, k, p = to // (members * pair), to // pair % members, to % pair
    order = jnp.where(source == k * table_rows + e * pair + p, 1.0, 0.0).astype(BF)
    return jnp.dot(order, stacked, preferred_element_type=F32).astype(BF)[:, : members * FOLD]


def route_body(members, experts, pair, _, *refs):
    count = len(refs) // 2
    packed, outs = refs[:count], refs[count:]
    width = outs[0].shape[1]
    half = width // 2

    def first():
        block = members * pair
        for side in range(2):
            cols = slice(side * half, (side + 1) * half)
            pick = tables_of(packed[:members], experts, pair, width, side)
            rows = jnp.concatenate(
                [part for ref in packed[:members] for part in (ref[:, cols], ref[:, width : width + half])], 0
            )
            got = jnp.dot(pick, rows, preferred_element_type=F32).astype(BF)
            for j in range(experts):
                outs[j][:block, cols] = got[j * block : (j + 1) * block]

    def second():
        rows = jnp.concatenate([ref[:, :width].astype(F32)[:pair] for ref in packed[:experts]], 0).astype(BF)
        for k in range(members):
            outs[k][: experts * pair] = rows

    by_core(first, second)


def weigh_body(experts, pair, width, *refs):
    packed, out = refs[:-1], refs[-1]
    out[...] = jnp.concatenate([tables_of(packed, experts, pair, width, g) for g in (2, 3, 4)], 1)


def weight_copies(source, target, sems, first):
    size = target.shape[0] // PIECES
    return [
        pltpu.make_async_copy(source.at[0, pl.ds(p * size, size)], target.at[pl.ds(p * size, size)], sems.at[first + p])
        for p in range(PIECES)
    ]


def fetch_body(count, *refs):
    sources, targets, sems = refs[:count], refs[count + 1 : -1], refs[-1]
    copies = []
    for i, (source, target) in enumerate(zip(sources, targets)):
        copies += weight_copies(source, target, sems, i * PIECES)
    for copy in copies:
        copy.start()
    for copy in copies:
        copy.wait()


def fetch(weights, after, name):
    return call(
        functools.partial(fetch_body, len(weights)),
        [pltpu.VMEM(w.shape[1:], BF) for w in weights],
        (*[pinned(w) for w in weights], after),
        name,
        [pltpu.HBM] * len(weights) + [pl.ANY],
        [pltpu.SemaphoreType.DMA((PIECES * len(weights),))],
        limit=1,
        moved=sum(2 * w.size for w in weights),
    )


def up_body(members, experts, pair, *refs):
    count = (len(refs) - 7) // 2
    mine, theirs, refs = refs[:count], refs[count : 2 * count], refs[2 * count :]
    gate_ref, up_ref, down_hbm, hidden_ref, down_ref, rows_ref, sems = refs
    copies = weight_copies(down_hbm, down_ref, sems, 0)
    for copy in copies:
        copy.start()

    def parts(core, blocks):
        number, size = ((experts, members * pair), (members, experts * pair))[core]
        return [b[:size] for b in blocks[:number]]

    def fill(core):
        rows_ref[...] = jnp.concatenate(parts(core, mine) + parts(1 - core, theirs), 0)

    if members == experts:
        fill(0)
    else:
        by_core(lambda: fill(0), lambda: fill(1))
    for j in range(hidden_ref.shape[1] // UNIT_TILE):
        cols = slice(j * UNIT_TILE, (j + 1) * UNIT_TILE)
        gate = jnp.dot(rows_ref[...], gate_ref[:, cols], preferred_element_type=F32)
        up = jnp.dot(rows_ref[...], up_ref[:, cols], preferred_element_type=F32)
        hidden_ref[:, cols] = (jax.nn.silu(gate) * up).astype(BF)
    for copy in copies:
        copy.wait()


def down_body(part, hidden_ref, down_ref, own_ref, other_ref):
    mine, width = own_ref.shape
    tile = min(512, width)
    for j in range(width // tile):
        cols = slice(j * tile, (j + 1) * tile)
        at = slice(part * width + j * tile, part * width + (j + 1) * tile)
        value = jnp.dot(hidden_ref[...], down_ref[:, at], preferred_element_type=F32).astype(BF)
        own_ref[:, cols] = value[:mine]
        other_ref[:, cols] = value[mine:]


def add_body(members, experts, pair, *refs):
    owns, gots, outs = refs[:PARTS], refs[PARTS : 2 * PARTS], refs[2 * PARTS :]
    width = owns[0].shape[1]

    def split(core):
        number, size = ((experts, members * pair), (members, experts * pair))[core]
        for j in range(number):
            at = slice(j * size, (j + 1) * size)
            for p in range(PARTS):
                cols = slice(p * width, (p + 1) * width)
                outs[j][:size, cols] = (owns[p][at].astype(F32) + gots[p][at].astype(F32)).astype(BF)

    if members == experts:
        split(0)
    else:
        by_core(lambda: split(0), lambda: split(1))


def blend_body(members, experts, pair, weights_ref, *refs):
    count = len(refs) // 2
    values, outs = refs[:count], refs[count:]
    width = values[0].shape[1]
    half = width // 2

    def first():
        tails = []
        for side in range(2):
            cols = slice(side * half, (side + 1) * half)
            value = jnp.concatenate([v[: members * pair, cols] for v in values[:experts]], 0)
            total = weigh_rows(weights_ref[...], value, members * FOLD)
            for k in range(members):
                outs[k][:, cols] = total[k * FOLD : k * FOLD + SUB].astype(BF)
            tails.append([total[k * FOLD + SUB : k * FOLD + SUB + 4] for k in range(members)])
        for k in range(members):
            outs[k][:, width:] = jnp.concatenate([tails[0][k], tails[1][k]], 0).astype(BF)

    def second():
        total = values[0][: experts * pair].astype(F32)
        for v in values[1:members]:
            total = total + v[: experts * pair].astype(F32)
        for j in range(experts):
            outs[j][:, :width] = padded(total[j * pair : (j + 1) * pair]).astype(BF)
            outs[j][:, width:] = jnp.zeros((SUB, half), BF)

    by_core(first, second)


def finish_body(members, experts, pair, table_ref, *refs):
    parts, out_ref = refs[:-1], refs[-1]
    rows, steps, width = out_ref.shape
    half = width // 2

    def write(flat):
        for r in range(rows):
            out_ref[r] = flat[r * steps : (r + 1) * steps].astype(BF)

    def first():
        total = parts[0][...].astype(F32)
        for p in parts[1:members]:
            total = total + p[...].astype(F32)
        tail = total[:, width:]
        tail = jnp.concatenate([tail[:4], tail[4:]], 1)
        write(jnp.concatenate([total[:, :width], tail], 0))

    def second():
        value = jnp.concatenate([p[:, :width].astype(F32)[:pair] for p in parts[:experts]], 0).astype(BF)
        write(weigh_rows(table_ref[:, 2 * FOLD : 5 * FOLD], value, FOLD))

    by_core(first, second)


def local(expert_input, expert_ids, combine, gate_weight, up_weight, down_weight):
    members = lax.axis_size("group")
    devices = lax.axis_size("dev")
    experts = devices // 2
    steps, row_count, width = expert_input.shape
    slots = max(2, (2 * row_count + experts - 1) // experts)
    pair = steps * slots
    folded = width + width // 2
    table_rows = experts * pair
    packed_width = folded + table_rows // SUB * LANES
    count = max(members, experts)
    block = count * pair
    rows_half = members * experts * pair
    hidden_units = gate_weight.shape[2]

    def send(arrays, group_core, back):
        got = {0: arrays[0]}
        for i in sorted(range(1, count), key=lambda i: -min(i, count - i)):
            pairs = []
            for g in range(members):
                for d in range(devices):
                    if d % 2 == group_core:
                        if i < members:
                            pairs.append((g * devices + d, (g + (-i if back else i)) % members * devices + d))
                    elif i < experts:
                        pairs.append((g * devices + d, g * devices + (d ^ (2 * i))))
            got[i] = lax.ppermute(arrays[i], ("group", "dev"), pairs)
        return [got[i] for i in range(count)]

    def swap(array):
        return lax.ppermute(array, "dev", [(i, i ^ 1) for i in range(devices)])

    x = expert_input.transpose(1, 0, 2)
    ids = expert_ids.transpose(0, 2, 1)
    scale = combine.transpose(0, 2, 1)
    *packed, table = call(
        functools.partial(pack_body, experts, slots),
        [(SUB, packed_width)] * count + [(table_rows, LANES)],
        [pinned(a) for a in (ids, scale, x)],
        "pack",
        [pltpu.HBM] * 3,
        [
            pltpu.SMEM(ids.shape, ids.dtype),
            pltpu.SMEM(scale.shape, scale.dtype),
            pltpu.VMEM(x.shape, x.dtype),
            pltpu.SemaphoreType.DMA((3,)),
        ],
    )
    (gate,) = fetch([gate_weight], packed[0], "fetch_gate")
    arrived = send(packed, 0, False)
    routed = call(
        functools.partial(route_body, members, experts, pair),
        [(block, width)] * count,
        (gate, *arrived),
        "route",
        [pl.ANY] + [pltpu.VMEM] * count,
    )
    (up,) = fetch([up_weight], routed[0], "fetch_up")
    mine = send(routed, 1, False)
    mine[-1], up = lax.optimization_barrier((mine[-1], up))
    theirs = [swap(a) for a in mine]
    (weights,) = call(
        functools.partial(weigh_body, experts, pair, width),
        [(rows_half, 3 * members * FOLD)],
        arrived[:members],
        "weigh",
    )
    hidden, down = call(
        functools.partial(up_body, members, experts, pair),
        [(2 * rows_half, hidden_units), pltpu.VMEM(down_weight.shape[1:], BF)],
        (*mine, *theirs, gate, up, pinned(down_weight)),
        "gate_up",
        [pltpu.VMEM] * (2 * count + 2) + [pltpu.HBM],
        scratch=[pltpu.VMEM((2 * rows_half, width), BF), pltpu.SemaphoreType.DMA((PIECES,))],
        flops=8 * rows_half * width * hidden_units,
    )
    owns, others = [], []
    for p in range(PARTS):
        own, other = call(
            functools.partial(down_body, p),
            [(rows_half, width // PARTS)] * 2,
            (hidden, down),
            "down_%d" % p,
            flops=4 * rows_half * width * hidden_units // PARTS,
        )
        owns.append(own)
        others.append(swap(other))
    halves = call(
        functools.partial(add_body, members, experts, pair), [(block, width)] * count, (*owns, *others), "add"
    )
    returned = send(halves, 1, True)
    blended = call(
        functools.partial(blend_body, members, experts, pair), [(SUB, folded)] * count, (weights, *returned), "blend"
    )
    final = send(blended, 0, True)
    (out,) = call(
        functools.partial(finish_body, members, experts, pair), [(row_count, steps, width)], (table, *final), "finish"
    )
    return out.transpose(1, 0, 2)


def solution(mesh):
    in_specs = (
        P(None, ("group", "dev"), None),
        P(None, ("group", "dev"), None),
        P(None, ("group", "dev"), None),
        P("dev", None, "group"),
        P("dev", None, "group"),
        P("dev", "group", None),
    )
    out_specs = P(None, ("group", "dev"), None)
    return jax.shard_map(local, mesh=mesh, in_specs=in_specs, out_specs=out_specs, check_vma=False)
```

```python
import functools

import jax
import jax.numpy as jnp
from jax import lax
from jax.experimental import pallas as pl
from jax.experimental.pallas import tpu as pltpu
from jax.sharding import PartitionSpec as P

BF = jnp.bfloat16
F32 = jnp.float32
LANES = 128
SUB = 8
FOLD = 16
UNIT_TILE = 256
CUTS = (0, 3, 4)
BESIDE_TRANSFER = 10**10


def group_peer(g, i, members, back):
    if members & (members - 1) == 0:
        return g ^ (-i % members)
    return (g + (-i if back else i)) % members


def plane_order(experts):
    return [0] + sorted(range(1, experts), key=lambda j: (-bin(j).count("1"), j))


def whole(memory_space=pltpu.VMEM):
    return pl.BlockSpec(memory_space=memory_space)


def pinned(array):
    return pltpu.with_memory_space_constraint(array, pltpu.HBM)


def call(body, outs, args, name, spaces=None, scratch=(), limit=12, flops=0):
    spaces = spaces or [pltpu.VMEM] * len(args)
    return pl.pallas_call(
        body,
        out_shape=[jax.ShapeDtypeStruct(s, BF) if isinstance(s, tuple) else s for s in outs],
        in_specs=[whole(s) for s in spaces],
        out_specs=[whole() for _ in outs],
        scratch_shapes=list(scratch),
        name=name,
        compiler_params=pltpu.CompilerParams(vmem_limit_bytes=limit << 20),
        cost_estimate=pl.CostEstimate(flops=flops, bytes_accessed=0, transcendentals=0),
    )(*args)


def by_core(first, second):
    core = lax.axis_index("dev") % 2
    pl.when(core == 0)(first)
    pl.when(core == 1)(second)


def padded(rows):
    missing = -rows.shape[0] % SUB
    return jnp.concatenate([rows, jnp.zeros((missing, rows.shape[1]), rows.dtype)], 0) if missing else rows


def weigh_rows(weights, value, span):
    total = lax.dot_general(weights, value, (((0,), (0,)), ((), ())), preferred_element_type=F32)
    return total[:span] + total[span : 2 * span] + total[2 * span :]


def pack_body(experts, slots, ids_hbm, combine_hbm, x_hbm, *refs):
    outs, table_out, (ids_ref, combine_ref, x_ref, sems) = refs[:-5], refs[-5], refs[-4:]
    copies = [
        pltpu.make_async_copy(source, target, sems.at[i])
        for i, (source, target) in enumerate(((ids_hbm, ids_ref), (combine_hbm, combine_ref), (x_hbm, x_ref)))
    ]
    for copy in copies:
        copy.start()
    rows, steps, width = x_ref.shape
    half = width // 2
    pair = steps * slots
    own = lax.axis_index("dev") // 2
    offsets = plane_order(experts)
    table_rows = experts * pair
    row_at = lax.broadcasted_iota(jnp.int32, (table_rows, LANES), 0)
    lane = lax.broadcasted_iota(jnp.int32, (table_rows, LANES), 1)
    group, place = lane // FOLD, lane % FOLD
    low = jnp.where((group == 1) & (place >= 12), place - 4, jnp.where((group == 1) & (place >= SUB), -1, place))
    table = jnp.zeros((table_rows, LANES), F32)
    copies[0].wait()
    copies[1].wait()
    for t in range(steps):
        counts = [jnp.int32(0)] * experts
        for r in range(rows):
            for k in range(2):
                e = ids_ref[t, k, r]
                position = jnp.int32(0)
                for c in range(experts):
                    position = jnp.where(e == c, counts[c], position)
                counts = [counts[c] + (e == c).astype(jnp.int32) for c in range(experts)]
                turn = sum(jnp.where((e ^ own) == offset, j, 0) for j, offset in enumerate(offsets))
                slot = (turn * steps + t) * slots + position
                hit = (row_at == slot) & (low == r * steps + t)
                table = jnp.where(hit, combine_ref[t, k, r], table)
    ones = jnp.where(table != 0.0, 1.0, 0.0)
    high = table.astype(BF).astype(F32)
    middle = (table - high).astype(BF).astype(F32)
    rest = table - high - middle
    coded = jnp.where(
        group <= 1, ones, jnp.where(group == 2, high, jnp.where(group == 3, middle, jnp.where(group == 4, rest, 0.0)))
    ).astype(BF)
    table_out[...] = coded
    copies[2].wait()
    flat = jnp.concatenate([x_ref[r].astype(F32) for r in range(rows)], 0)

    def first():
        tail = flat[SUB:]
        top = flat[:SUB].astype(BF)
        fold = jnp.concatenate([tail[:, :half], tail[:, half:]], 0).astype(BF)
        for out in outs:
            out[:, :width] = top
            out[:, width : width + half] = fold
            for b in range(table_rows // SUB):
                start = width + half + b * LANES
                out[:, start : start + LANES] = coded[b * SUB : (b + 1) * SUB]

    def second():
        source = jnp.concatenate([flat, jnp.zeros((FOLD - flat.shape[0], width), F32)], 0).astype(BF)
        got = jnp.dot(coded[:, :FOLD], source, preferred_element_type=F32)
        for j, out in enumerate(outs):
            if j < experts:
                out[:, :width] = padded(got[j * pair : (j + 1) * pair]).astype(BF)
            else:
                out[:, :width] = jnp.zeros((SUB, width), BF)
            out[:, width:] = jnp.zeros((SUB, out.shape[1] - width), BF)

    by_core(first, second)


def tables_of(packed, experts, pair, width, groups):
    base = width + width // 2
    members = len(packed)
    table_rows = experts * pair
    total = table_rows * members
    span = -(-members * FOLD // LANES) * LANES
    blocks = []
    for k, ref in enumerate(packed):
        tab = jnp.concatenate(
            [ref[:, base + b * LANES : base + (b + 1) * LANES] for b in range(table_rows // SUB)], 0
        ).astype(F32)
        at = k % (LANES // FOLD)
        here = lax.broadcasted_iota(jnp.int32, tab.shape, 1) // FOLD == at
        tiles = []
        for group in groups:
            shift = (at - group) * FOLD % LANES
            moved = jnp.where(here, pltpu.roll(tab, shift, 1) if shift else tab, 0.0)
            row = [jnp.zeros_like(moved)] * (span // LANES)
            row[k * FOLD // LANES] = moved
            tiles += row
        blocks.append(jnp.concatenate(tiles, 1))
    stacked = jnp.concatenate(blocks, 0).astype(BF)
    to = lax.broadcasted_iota(jnp.int32, (total, total), 0)
    source = lax.broadcasted_iota(jnp.int32, (total, total), 1)
    e, k, p = to // (members * pair), to // pair % members, to % pair
    order = jnp.where(source == k * table_rows + e * pair + p, 1.0, 0.0).astype(BF)
    all_groups = jnp.dot(order, stacked, preferred_element_type=F32).astype(BF)
    return [all_groups[:, i * span : i * span + members * FOLD] for i in range(len(groups))]


def route_body(members, experts, pair, *refs):
    count = len(refs) // 2
    packed, outs = refs[:count], refs[count:]
    width = outs[0].shape[1]
    half = width // 2

    def first():
        block = members * pair
        for side, pick in enumerate(tables_of(packed[:members], experts, pair, width, (0, 1))):
            cols = slice(side * half, (side + 1) * half)
            rows = jnp.concatenate(
                [part for ref in packed[:members] for part in (ref[:, cols], ref[:, width : width + half])], 0
            )
            got = jnp.dot(pick, rows, preferred_element_type=F32).astype(BF)
            for j in range(experts):
                outs[j][:block, cols] = got[j * block : (j + 1) * block]

    def second():
        rows = jnp.concatenate([ref[:, :width].astype(F32)[:pair] for ref in packed[:experts]], 0).astype(BF)
        for k in range(members):
            outs[k][: experts * pair] = rows

    by_core(first, second)


def weigh_body(experts, pair, width, *refs):
    packed, out = refs[:-1], refs[-1]
    out[...] = jnp.concatenate(tables_of(packed, experts, pair, width, (2, 3, 4)), 1)


def up_body(members, experts, pair, *refs):
    count = (len(refs) - 4) // 2
    mine, theirs, refs = refs[:count], refs[count : 2 * count], refs[2 * count :]
    gate_ref, up_ref, hidden_ref, rows_ref = refs

    def parts(core, blocks):
        number, size = ((experts, members * pair), (members, experts * pair))[core]
        return [b[:size] for b in blocks[:number]]

    def fill(core):
        rows_ref[...] = jnp.concatenate(parts(core, mine) + parts(1 - core, theirs), 0)

    if members == experts:
        fill(0)
    else:
        by_core(lambda: fill(0), lambda: fill(1))
    for j in range(hidden_ref.shape[1] // UNIT_TILE):
        cols = slice(j * UNIT_TILE, (j + 1) * UNIT_TILE)
        gate = jnp.dot(rows_ref[...], gate_ref[:, cols], preferred_element_type=F32)
        up = jnp.dot(rows_ref[...], up_ref[:, cols], preferred_element_type=F32)
        hidden_ref[:, cols] = (jax.nn.silu(gate) * up).astype(BF)


def down_body(first, hidden_ref, down_ref, own_ref, other_ref):
    mine, width = own_ref.shape
    tile = min(512, width)
    for j in range(width // tile):
        cols = slice(j * tile, (j + 1) * tile)
        at = slice(first + j * tile, first + (j + 1) * tile)
        value = jnp.dot(hidden_ref[...], down_ref[:, at], preferred_element_type=F32).astype(BF)
        own_ref[:, cols] = value[:mine]
        other_ref[:, cols] = value[mine:]


def add_body(members, experts, pair, *refs):
    parts = len(CUTS) - 1
    owns, gots, outs = refs[:parts], refs[parts : 2 * parts], refs[2 * parts :]

    def split(core):
        number, size = ((experts, members * pair), (members, experts * pair))[core]
        for j in range(number):
            at = slice(j * size, (j + 1) * size)
            first = 0
            for own_ref, got_ref in zip(owns, gots):
                cols = slice(first, first + own_ref.shape[1])
                outs[j][:size, cols] = (own_ref[at].astype(F32) + got_ref[at].astype(F32)).astype(BF)
                first += own_ref.shape[1]

    if members == experts:
        split(0)
    else:
        by_core(lambda: split(0), lambda: split(1))


def blend_body(members, experts, pair, weights_ref, *refs):
    count = len(refs) // 2
    values, outs = refs[:count], refs[count:]
    width = values[0].shape[1]
    half = width // 2

    def first():
        tails = []
        for side in range(2):
            cols = slice(side * half, (side + 1) * half)
            value = jnp.concatenate([v[: members * pair, cols] for v in values[:experts]], 0)
            total = weigh_rows(weights_ref[...], value, members * FOLD)
            for k in range(members):
                outs[k][:, cols] = total[k * FOLD : k * FOLD + SUB].astype(BF)
            tails.append([total[k * FOLD + SUB : k * FOLD + SUB + 4] for k in range(members)])
        for k in range(members):
            outs[k][:, width:] = jnp.concatenate([tails[0][k], tails[1][k]], 0).astype(BF)

    def second():
        total = values[0][: experts * pair].astype(F32)
        for v in values[1:members]:
            total = total + v[: experts * pair].astype(F32)
        for j in range(experts):
            outs[j][:, :width] = padded(total[j * pair : (j + 1) * pair]).astype(BF)
            outs[j][:, width:] = jnp.zeros((SUB, half), BF)

    by_core(first, second)


def finish_body(members, experts, pair, table_ref, *refs):
    parts, out_ref = refs[:-1], refs[-1]
    rows, steps, width = out_ref.shape
    half = width // 2

    def write(flat):
        for r in range(rows):
            out_ref[r] = flat[r * steps : (r + 1) * steps].astype(BF)

    def first():
        total = parts[0][...].astype(F32)
        for p in parts[1:members]:
            total = total + p[...].astype(F32)
        tail = total[:, width:]
        tail = jnp.concatenate([tail[:4], tail[4:]], 1)
        write(jnp.concatenate([total[:, :width], tail], 0))

    def second():
        value = jnp.concatenate([p[:, :width].astype(F32)[:pair] for p in parts[:experts]], 0).astype(BF)
        write(weigh_rows(table_ref[:, 2 * FOLD : 5 * FOLD], value, FOLD))

    by_core(first, second)


def local(expert_input, expert_ids, combine, gate_weight, up_weight, down_weight):
    members = lax.axis_size("group")
    devices = lax.axis_size("dev")
    experts = devices // 2
    steps, row_count, width = expert_input.shape
    slots = max(2, (2 * row_count + experts - 1) // experts)
    pair = steps * slots
    folded = width + width // 2
    table_rows = experts * pair
    packed_width = folded + table_rows // SUB * LANES
    count = max(members, experts)
    block = count * pair
    rows_half = members * experts * pair
    hidden_units = gate_weight.shape[2]

    offsets = plane_order(experts)

    def send(arrays, group_core, back):
        got = {0: arrays[0]}
        for i in sorted(range(1, count), key=lambda i: -min(i, count - i)):
            pairs = []
            for g in range(members):
                for d in range(devices):
                    if d % 2 == group_core:
                        if i < members:
                            pairs.append((g * devices + d, group_peer(g, i, members, back) * devices + d))
                    elif i < experts:
                        pairs.append((g * devices + d, g * devices + (d ^ (2 * offsets[i]))))
            got[i] = lax.ppermute(arrays[i], ("group", "dev"), pairs)
        return [got[i] for i in range(count)]

    def swap(array):
        return lax.ppermute(array, "dev", [(i, i ^ 1) for i in range(devices)])

    x = expert_input.transpose(1, 0, 2)
    ids = expert_ids.transpose(0, 2, 1)
    scale = combine.transpose(0, 2, 1)
    *packed, table = call(
        functools.partial(pack_body, experts, slots),
        [(SUB, packed_width)] * count + [(table_rows, LANES)],
        [pinned(a) for a in (ids, scale, x)],
        "pack",
        [pltpu.HBM] * 3,
        [
            pltpu.SMEM(ids.shape, ids.dtype),
            pltpu.SMEM(scale.shape, scale.dtype),
            pltpu.VMEM(x.shape, x.dtype),
            pltpu.SemaphoreType.DMA((3,)),
        ],
        flops=BESIDE_TRANSFER,
    )
    arrived = send(packed, 0, False)
    routed = call(
        functools.partial(route_body, members, experts, pair),
        [(block, width)] * count,
        arrived,
        "route",
        flops=BESIDE_TRANSFER,
    )
    mine = send(routed, 1, False)
    theirs = [swap(a) for a in mine]
    (weights,) = call(
        functools.partial(weigh_body, experts, pair, width),
        [(rows_half, 3 * members * FOLD)],
        arrived[:members],
        "weigh",
    )
    (hidden,) = call(
        functools.partial(up_body, members, experts, pair),
        [(2 * rows_half, hidden_units)],
        (*mine, *theirs, gate_weight[0], up_weight[0]),
        "gate_up",
        [pltpu.VMEM] * (2 * count + 2),
        scratch=[pltpu.VMEM((2 * rows_half, width), BF)],
        flops=8 * rows_half * width * hidden_units,
    )
    owns, others = [], []
    for p, (low, high) in enumerate(zip(CUTS, CUTS[1:])):
        low, high = low * width // CUTS[-1], high * width // CUTS[-1]
        own, other = call(
            functools.partial(down_body, low),
            [(rows_half, high - low)] * 2,
            (hidden, down_weight[0]),
            "down_%d" % p,
            flops=4 * rows_half * (high - low) * hidden_units,
        )
        owns.append(own)
        others.append(swap(other))
    halves = call(
        functools.partial(add_body, members, experts, pair), [(block, width)] * count, (*owns, *others), "add"
    )
    returned = send(halves, 1, True)
    blended = call(
        functools.partial(blend_body, members, experts, pair), [(SUB, folded)] * count, (weights, *returned), "blend"
    )
    final = send(blended, 0, True)
    (out,) = call(
        functools.partial(finish_body, members, experts, pair), [(row_count, steps, width)], (table, *final), "finish"
    )
    return out.transpose(1, 0, 2)


def solution(mesh):
    in_specs = (
        P(None, ("group", "dev"), None),
        P(None, ("group", "dev"), None),
        P(None, ("group", "dev"), None),
        P("dev", None, "group"),
        P("dev", None, "group"),
        P("dev", "group", None),
    )
    out_specs = P(None, ("group", "dev"), None)
    return jax.shard_map(local, mesh=mesh, in_specs=in_specs, out_specs=out_specs, check_vma=False)
```

```python
import functools

import jax
import jax.numpy as jnp
from jax import lax
from jax.experimental import pallas as pl
from jax.experimental.pallas import tpu as pltpu
from jax.sharding import PartitionSpec as P

BF = jnp.bfloat16
F32 = jnp.float32
LANES = 128
SUB = 8
FOLD = 16
UNIT_TILE = 256
CUTS = (0, 3, 4)
BESIDE_TRANSFER = 10**10


def group_peer(g, i, members, back):
    ring = [n ^ (n >> 1) for n in range(members)]
    if sorted(ring) != list(range(members)):
        ring = list(range(members))
    return ring[(ring.index(g) + (i if back else -i)) % members]


def plane_order(experts):
    return [0] + sorted(range(1, experts), key=lambda j: (-bin(j).count("1"), j))


def whole(memory_space=pltpu.VMEM):
    return pl.BlockSpec(memory_space=memory_space)


def pinned(array):
    return pltpu.with_memory_space_constraint(array, pltpu.HBM)


def call(body, outs, args, name, spaces=None, scratch=(), limit=12, flops=0):
    spaces = spaces or [pltpu.VMEM] * len(args)
    return pl.pallas_call(
        body,
        out_shape=[jax.ShapeDtypeStruct(s, BF) if isinstance(s, tuple) else s for s in outs],
        in_specs=[whole(s) for s in spaces],
        out_specs=[whole() for _ in outs],
        scratch_shapes=list(scratch),
        name=name,
        compiler_params=pltpu.CompilerParams(vmem_limit_bytes=limit << 20),
        cost_estimate=pl.CostEstimate(flops=flops, bytes_accessed=0, transcendentals=0),
    )(*args)


def by_core(first, second):
    core = lax.axis_index("dev") % 2
    pl.when(core == 0)(first)
    pl.when(core == 1)(second)


def padded(rows):
    missing = -rows.shape[0] % SUB
    return jnp.concatenate([rows, jnp.zeros((missing, rows.shape[1]), rows.dtype)], 0) if missing else rows


def weigh_rows(weights, value, span):
    total = jnp.dot(weights, value, preferred_element_type=F32)
    return total[:span] + total[span : 2 * span] + total[2 * span :]


def pack_body(experts, slots, ids_hbm, combine_hbm, x_hbm, *refs):
    outs, table_out, (ids_ref, combine_ref, x_ref, sems) = refs[:-5], refs[-5], refs[-4:]
    copies = [
        pltpu.make_async_copy(source, target, sems.at[i])
        for i, (source, target) in enumerate(((ids_hbm, ids_ref), (combine_hbm, combine_ref), (x_hbm, x_ref)))
    ]
    for copy in copies:
        copy.start()
    rows, steps, width = x_ref.shape
    half = width // 2
    pair = steps * slots
    own = lax.axis_index("dev") // 2
    offsets = plane_order(experts)
    table_rows = experts * pair
    row_at = lax.broadcasted_iota(jnp.int32, (table_rows, LANES), 0)
    lane = lax.broadcasted_iota(jnp.int32, (table_rows, LANES), 1)
    group, place = lane // FOLD, lane % FOLD
    low = jnp.where((group == 1) & (place >= 12), place - 4, jnp.where((group == 1) & (place >= SUB), -1, place))
    table = jnp.zeros((table_rows, LANES), F32)
    copies[0].wait()
    copies[1].wait()
    turns = sum(offsets.index(offset) << (4 * offset) for offset in range(experts))
    turns = jnp.int32(turns - (1 << 32) if turns >> 31 else turns)
    for t in range(steps):
        counts = jnp.int32(0)
        for r in range(rows):
            for k in range(2):
                e = ids_ref[t, k, r]
                position = (counts >> (4 * e)) & 15
                counts = counts + (1 << (4 * e))
                turn = (turns >> (4 * (e ^ own))) & 15
                slot = (turn * steps + t) * slots + position
                hit = (row_at == slot) & (low == r * steps + t)
                table = jnp.where(hit, combine_ref[t, k, r], table)
    ones = jnp.where(table != 0.0, 1.0, 0.0)
    high = table.astype(BF).astype(F32)
    middle = (table - high).astype(BF).astype(F32)
    rest = table - high - middle
    coded = jnp.where(
        group <= 1, ones, jnp.where(group == 2, high, jnp.where(group == 3, middle, jnp.where(group == 4, rest, 0.0)))
    ).astype(BF)
    table_out[...] = coded
    copies[2].wait()
    flat = jnp.concatenate([x_ref[r].astype(F32) for r in range(rows)], 0)

    def first():
        tail = flat[SUB:]
        top = flat[:SUB].astype(BF)
        fold = jnp.concatenate([tail[:, :half], tail[:, half:]], 0).astype(BF)
        for out in outs:
            out[:, :width] = top
            out[:, width : width + half] = fold
            for b in range(table_rows // SUB):
                start = width + half + b * LANES
                out[:, start : start + LANES] = coded[b * SUB : (b + 1) * SUB]

    def second():
        source = jnp.concatenate([flat, jnp.zeros((FOLD - flat.shape[0], width), F32)], 0).astype(BF)
        got = jnp.dot(coded[:, :FOLD], source, preferred_element_type=F32)
        for j, out in enumerate(outs):
            if j < experts:
                out[:, :width] = padded(got[j * pair : (j + 1) * pair]).astype(BF)
            else:
                out[:, :width] = jnp.zeros((SUB, width), BF)
            out[:, width:] = jnp.zeros((SUB, out.shape[1] - width), BF)

    by_core(first, second)


def tables_of(packed, experts, pair, width, groups):
    base = width + width // 2
    members = len(packed)
    table_rows = experts * pair
    total = table_rows * members
    span = -(-members * FOLD // LANES) * LANES
    blocks = []
    for k, ref in enumerate(packed):
        tab = jnp.concatenate(
            [ref[:, base + b * LANES : base + (b + 1) * LANES] for b in range(table_rows // SUB)], 0
        ).astype(F32)
        at = k % (LANES // FOLD)
        here = lax.broadcasted_iota(jnp.int32, tab.shape, 1) // FOLD == at
        tiles = []
        for group in groups:
            shift = (at - group) * FOLD % LANES
            moved = jnp.where(here, pltpu.roll(tab, shift, 1) if shift else tab, 0.0)
            row = [jnp.zeros_like(moved)] * (span // LANES)
            row[k * FOLD // LANES] = moved
            tiles += row
        blocks.append(jnp.concatenate(tiles, 1))
    stacked = jnp.concatenate(blocks, 0).astype(BF)
    to = lax.broadcasted_iota(jnp.int32, (total, total), 0)
    source = lax.broadcasted_iota(jnp.int32, (total, total), 1)
    e, k, p = to // (members * pair), to // pair % members, to % pair
    order = jnp.where(source == k * table_rows + e * pair + p, 1.0, 0.0).astype(BF)
    all_groups = jnp.dot(order, stacked, preferred_element_type=F32).astype(BF)
    return [all_groups[:, i * span : i * span + members * FOLD] for i in range(len(groups))]


def route_body(members, experts, pair, *refs):
    count = len(refs) // 2
    packed, outs = refs[:count], refs[count:]
    width = outs[0].shape[1]
    half = width // 2

    def first():
        block = members * pair
        for side, pick in enumerate(tables_of(packed[:members], experts, pair, width, (0, 1))):
            cols = slice(side * half, (side + 1) * half)
            rows = jnp.concatenate(
                [part for ref in packed[:members] for part in (ref[:, cols], ref[:, width : width + half])], 0
            )
            got = jnp.dot(pick, rows, preferred_element_type=F32).astype(BF)
            for j in range(experts):
                outs[j][:block, cols] = got[j * block : (j + 1) * block]

    def second():
        rows = jnp.concatenate([ref[:, :width].astype(F32)[:pair] for ref in packed[:experts]], 0).astype(BF)
        for k in range(members):
            outs[k][: experts * pair] = rows

    by_core(first, second)


def weigh_body(experts, pair, width, *refs):
    packed, out = refs[:-1], refs[-1]
    tables = tables_of(packed, experts, pair, width, (2, 3, 4))
    out[...] = jnp.concatenate([t.astype(F32).T for t in tables], 0).astype(BF)


def up_body(members, experts, pair, *refs):
    count = (len(refs) - 4) // 2
    mine, theirs, refs = refs[:count], refs[count : 2 * count], refs[2 * count :]
    gate_ref, up_ref, hidden_ref, rows_ref = refs

    def parts(core, blocks):
        number, size = ((experts, members * pair), (members, experts * pair))[core]
        return [b[:size] for b in blocks[:number]]

    def fill(core):
        rows_ref[...] = jnp.concatenate(parts(core, mine) + parts(1 - core, theirs), 0)

    if members == experts:
        fill(0)
    else:
        by_core(lambda: fill(0), lambda: fill(1))
    for j in range(hidden_ref.shape[1] // UNIT_TILE):
        cols = slice(j * UNIT_TILE, (j + 1) * UNIT_TILE)
        gate = jnp.dot(rows_ref[...], gate_ref[:, cols], preferred_element_type=F32)
        up = jnp.dot(rows_ref[...], up_ref[:, cols], preferred_element_type=F32)
        hidden_ref[:, cols] = (jax.nn.silu(gate) * up).astype(BF)


def down_body(first, hidden_ref, down_ref, own_ref, other_ref):
    mine, width = own_ref.shape
    tile = min(512, width)
    for j in range(width // tile):
        cols = slice(j * tile, (j + 1) * tile)
        at = slice(first + j * tile, first + (j + 1) * tile)
        value = jnp.dot(hidden_ref[...], down_ref[:, at], preferred_element_type=F32).astype(BF)
        own_ref[:, cols] = value[:mine]
        other_ref[:, cols] = value[mine:]


def add_body(members, experts, pair, *refs):
    parts = len(CUTS) - 1
    owns, gots, outs = refs[:parts], refs[parts : 2 * parts], refs[2 * parts :]

    def split(core):
        number, size = ((experts, members * pair), (members, experts * pair))[core]
        for j in range(number):
            at = slice(j * size, (j + 1) * size)
            first = 0
            for own_ref, got_ref in zip(owns, gots):
                cols = slice(first, first + own_ref.shape[1])
                outs[j][:size, cols] = (own_ref[at].astype(F32) + got_ref[at].astype(F32)).astype(BF)
                first += own_ref.shape[1]

    if members == experts:
        split(0)
    else:
        by_core(lambda: split(0), lambda: split(1))


def blend_body(members, experts, pair, weights_ref, *refs):
    count = len(refs) // 2
    values, outs = refs[:count], refs[count:]
    width = values[0].shape[1]
    half = width // 2

    def first():
        tails = []
        for side in range(2):
            cols = slice(side * half, (side + 1) * half)
            value = jnp.concatenate([v[: members * pair, cols] for v in values[:experts]], 0)
            total = weigh_rows(weights_ref[...], value, members * FOLD)
            for k in range(members):
                outs[k][:, cols] = total[k * FOLD : k * FOLD + SUB].astype(BF)
            tails.append([total[k * FOLD + SUB : k * FOLD + SUB + 4] for k in range(members)])
        for k in range(members):
            outs[k][:, width:] = jnp.concatenate([tails[0][k], tails[1][k]], 0).astype(BF)

    def second():
        total = values[0][: experts * pair].astype(F32)
        for v in values[1:members]:
            total = total + v[: experts * pair].astype(F32)
        for j in range(experts):
            outs[j][:, :width] = padded(total[j * pair : (j + 1) * pair]).astype(BF)
            outs[j][:, width:] = jnp.zeros((SUB, half), BF)

    by_core(first, second)


def finish_body(members, experts, pair, table_ref, *refs):
    parts, out_ref = refs[:-1], refs[-1]
    rows, steps, width = out_ref.shape
    half = width // 2

    def write(flat):
        for r in range(rows):
            out_ref[r] = flat[r * steps : (r + 1) * steps].astype(BF)

    def first():
        total = parts[0][...].astype(F32)
        for p in parts[1:members]:
            total = total + p[...].astype(F32)
        tail = total[:, width:]
        tail = jnp.concatenate([tail[:4], tail[4:]], 1)
        write(jnp.concatenate([total[:, :width], tail], 0))

    def second():
        value = jnp.concatenate([p[:, :width].astype(F32)[:pair] for p in parts[:experts]], 0).astype(BF)
        write(weigh_rows(table_ref[:, 2 * FOLD : 5 * FOLD].astype(F32).T.astype(BF), value, FOLD))

    by_core(first, second)


def local(expert_input, expert_ids, combine, gate_weight, up_weight, down_weight):
    members = lax.axis_size("group")
    devices = lax.axis_size("dev")
    experts = devices // 2
    steps, row_count, width = expert_input.shape
    slots = max(2, (2 * row_count + experts - 1) // experts)
    pair = steps * slots
    folded = width + width // 2
    table_rows = experts * pair
    packed_width = folded + table_rows // SUB * LANES
    count = max(members, experts)
    block = count * pair
    rows_half = members * experts * pair
    hidden_units = gate_weight.shape[2]

    offsets = plane_order(experts)

    def send(arrays, group_core, back):
        got = {0: arrays[0]}
        for i in sorted(range(1, count), key=lambda i: -min(i, count - i)):
            pairs = []
            for g in range(members):
                for d in range(devices):
                    if d % 2 == group_core:
                        if i < members:
                            pairs.append((g * devices + d, group_peer(g, i, members, back) * devices + d))
                    elif i < experts:
                        pairs.append((g * devices + d, g * devices + (d ^ (2 * offsets[i]))))
            got[i] = lax.ppermute(arrays[i], ("group", "dev"), pairs)
        return [got[i] for i in range(count)]

    def swap(array):
        return lax.ppermute(array, "dev", [(i, i ^ 1) for i in range(devices)])

    x = expert_input.transpose(1, 0, 2)
    ids = expert_ids.transpose(0, 2, 1)
    scale = combine.transpose(0, 2, 1)
    *packed, table = call(
        functools.partial(pack_body, experts, slots),
        [(SUB, packed_width)] * count + [(table_rows, LANES)],
        [pinned(a) for a in (ids, scale, x)],
        "pack",
        [pltpu.HBM] * 3,
        [
            pltpu.SMEM(ids.shape, ids.dtype),
            pltpu.SMEM(scale.shape, scale.dtype),
            pltpu.VMEM(x.shape, x.dtype),
            pltpu.SemaphoreType.DMA((3,)),
        ],
        flops=BESIDE_TRANSFER,
    )
    arrived = send(packed, 0, False)
    routed = call(
        functools.partial(route_body, members, experts, pair),
        [(block, width)] * count,
        arrived,
        "route",
        flops=BESIDE_TRANSFER,
    )
    mine = send(routed, 1, False)
    theirs = [swap(a) for a in mine]
    (weights,) = call(
        functools.partial(weigh_body, experts, pair, width),
        [(3 * members * FOLD, rows_half)],
        arrived[:members],
        "weigh",
    )
    (hidden,) = call(
        functools.partial(up_body, members, experts, pair),
        [(2 * rows_half, hidden_units)],
        (*mine, *theirs, gate_weight[0], up_weight[0]),
        "gate_up",
        [pltpu.VMEM] * (2 * count + 2),
        scratch=[pltpu.VMEM((2 * rows_half, width), BF)],
        flops=8 * rows_half * width * hidden_units,
    )
    owns, others = [], []
    for p, (low, high) in enumerate(zip(CUTS, CUTS[1:])):
        low, high = low * width // CUTS[-1], high * width // CUTS[-1]
        own, other = call(
            functools.partial(down_body, low),
            [(rows_half, high - low)] * 2,
            (hidden, down_weight[0]),
            "down_%d" % p,
            flops=4 * rows_half * (high - low) * hidden_units,
        )
        owns.append(own)
        others.append(swap(other))
    halves = call(
        functools.partial(add_body, members, experts, pair), [(block, width)] * count, (*owns, *others), "add"
    )
    returned = send(halves, 1, True)
    blended = call(
        functools.partial(blend_body, members, experts, pair), [(SUB, folded)] * count, (weights, *returned), "blend"
    )
    final = send(blended, 0, True)
    (out,) = call(
        functools.partial(finish_body, members, experts, pair), [(row_count, steps, width)], (table, *final), "finish"
    )
    return out.transpose(1, 0, 2)


def solution(mesh):
    in_specs = (
        P(None, ("group", "dev"), None),
        P(None, ("group", "dev"), None),
        P(None, ("group", "dev"), None),
        P("dev", None, "group"),
        P("dev", None, "group"),
        P("dev", "group", None),
    )
    out_specs = P(None, ("group", "dev"), None)
    return jax.shard_map(local, mesh=mesh, in_specs=in_specs, out_specs=out_specs, check_vma=False)
```

```python
import functools

import jax
import jax.numpy as jnp
from jax import lax
from jax.experimental import pallas as pl
from jax.experimental.pallas import tpu as pltpu
from jax.sharding import PartitionSpec as P

BF = jnp.bfloat16
F32 = jnp.float32
LANES = 128
SUB = 8
FOLD = 16
UNIT_TILE = 256
CUTS = (0, 3, 4)
BESIDE_TRANSFER = 10**10


def group_peer(g, i, members, back):
    ring = [n ^ (n >> 1) for n in range(members)]
    if sorted(ring) != list(range(members)):
        ring = list(range(members))
    return ring[(ring.index(g) + (i if back else -i)) % members]


def plane_order(experts):
    return [0] + sorted(range(1, experts), key=lambda j: (-bin(j).count("1"), j))


def whole(memory_space=pltpu.VMEM):
    return pl.BlockSpec(memory_space=memory_space)


def pinned(array):
    return pltpu.with_memory_space_constraint(array, pltpu.HBM)


def call(body, outs, args, name, spaces=None, scratch=(), limit=12, flops=0):
    spaces = spaces or [pltpu.VMEM] * len(args)
    return pl.pallas_call(
        body,
        out_shape=[jax.ShapeDtypeStruct(s, BF) if isinstance(s, tuple) else s for s in outs],
        in_specs=[whole(s) for s in spaces],
        out_specs=[whole() for _ in outs],
        scratch_shapes=list(scratch),
        name=name,
        compiler_params=pltpu.CompilerParams(vmem_limit_bytes=limit << 20),
        cost_estimate=pl.CostEstimate(flops=flops, bytes_accessed=0, transcendentals=0),
    )(*args)


def by_core(first, second):
    core = lax.axis_index("dev") % 2
    pl.when(core == 0)(first)
    pl.when(core == 1)(second)


def padded(rows):
    missing = -rows.shape[0] % SUB
    return jnp.concatenate([rows, jnp.zeros((missing, rows.shape[1]), rows.dtype)], 0) if missing else rows


def weigh_rows(weights, value, span):
    total = jnp.dot(weights, value, preferred_element_type=F32)
    return total[:span] + total[span : 2 * span] + total[2 * span :]


def pack_body(experts, slots, ids_hbm, combine_hbm, x_hbm, *refs):
    outs, table_out, (ids_ref, combine_ref, x_ref, sems) = refs[:-5], refs[-5], refs[-4:]
    copies = [
        pltpu.make_async_copy(source, target, sems.at[i])
        for i, (source, target) in enumerate(((ids_hbm, ids_ref), (combine_hbm, combine_ref), (x_hbm, x_ref)))
    ]
    for copy in copies:
        copy.start()
    rows, steps, width = x_ref.shape
    half = width // 2
    pair = steps * slots
    own = lax.axis_index("dev") // 2
    offsets = plane_order(experts)
    table_rows = experts * pair
    row_at = lax.broadcasted_iota(jnp.int32, (table_rows, LANES), 0)
    lane = lax.broadcasted_iota(jnp.int32, (table_rows, LANES), 1)
    group, place = lane // FOLD, lane % FOLD
    low = jnp.where((group == 1) & (place >= 12), place - 4, jnp.where((group == 1) & (place >= SUB), -1, place))
    table = jnp.zeros((table_rows, LANES), F32)
    copies[0].wait()
    copies[1].wait()
    turns = sum(offsets.index(offset) << (4 * offset) for offset in range(experts))
    turns = jnp.int32(turns - (1 << 32) if turns >> 31 else turns)
    for t in range(steps):
        counts = jnp.int32(0)
        for r in range(rows):
            for k in range(2):
                e = ids_ref[t, k, r]
                position = (counts >> (4 * e)) & 15
                counts = counts + (1 << (4 * e))
                turn = (turns >> (4 * (e ^ own))) & 15
                slot = (turn * steps + t) * slots + position
                hit = (row_at == slot) & (low == r * steps + t)
                table = jnp.where(hit, combine_ref[t, k, r], table)
    ones = jnp.where(table != 0.0, 1.0, 0.0)
    high = table.astype(BF).astype(F32)
    middle = (table - high).astype(BF).astype(F32)
    rest = table - high - middle
    coded = jnp.where(
        group <= 1, ones, jnp.where(group == 2, high, jnp.where(group == 3, middle, jnp.where(group == 4, rest, 0.0)))
    ).astype(BF)
    table_out[...] = coded
    copies[2].wait()
    flat = jnp.concatenate([x_ref[r].astype(F32) for r in range(rows)], 0)

    def first():
        tail = flat[SUB:]
        top = flat[:SUB].astype(BF)
        fold = jnp.concatenate([tail[:, :half], tail[:, half:]], 0).astype(BF)
        for out in outs:
            out[:, :width] = top
            out[:, width : width + half] = fold
            for b in range(table_rows // SUB):
                start = width + half + b * LANES
                out[:, start : start + LANES] = coded[b * SUB : (b + 1) * SUB]

    def second():
        source = jnp.concatenate([flat, jnp.zeros((FOLD - flat.shape[0], width), F32)], 0).astype(BF)
        got = jnp.dot(coded[:, :FOLD], source, preferred_element_type=F32)
        for j, out in enumerate(outs):
            if j < experts:
                out[:, :width] = padded(got[j * pair : (j + 1) * pair]).astype(BF)
            else:
                out[:, :width] = jnp.zeros((SUB, width), BF)
            out[:, width:] = jnp.zeros((SUB, out.shape[1] - width), BF)

    by_core(first, second)


def tables_of(packed, experts, pair, width, groups):
    base = width + width // 2
    members = len(packed)
    table_rows = experts * pair
    total = table_rows * members
    span = -(-members * FOLD // LANES) * LANES
    blocks = []
    for k, ref in enumerate(packed):
        tab = jnp.concatenate(
            [ref[:, base + b * LANES : base + (b + 1) * LANES] for b in range(table_rows // SUB)], 0
        ).astype(F32)
        at = k % (LANES // FOLD)
        here = lax.broadcasted_iota(jnp.int32, tab.shape, 1) // FOLD == at
        tiles = []
        for group in groups:
            shift = (at - group) * FOLD % LANES
            moved = jnp.where(here, pltpu.roll(tab, shift, 1) if shift else tab, 0.0)
            row = [jnp.zeros_like(moved)] * (span // LANES)
            row[k * FOLD // LANES] = moved
            tiles += row
        blocks.append(jnp.concatenate(tiles, 1))
    stacked = jnp.concatenate(blocks, 0).astype(BF)
    to = lax.broadcasted_iota(jnp.int32, (total, total), 0)
    source = lax.broadcasted_iota(jnp.int32, (total, total), 1)
    e, k, p = to // (members * pair), to // pair % members, to % pair
    order = jnp.where(source == k * table_rows + e * pair + p, 1.0, 0.0).astype(BF)
    all_groups = jnp.dot(order, stacked, preferred_element_type=F32).astype(BF)
    return [all_groups[:, i * span : i * span + members * FOLD] for i in range(len(groups))]


def route_body(members, experts, pair, *refs):
    count = len(refs) // 2
    packed, outs = refs[:count], refs[count:]
    width = outs[0].shape[1]
    half = width // 2

    def first():
        block = members * pair
        for side, pick in enumerate(tables_of(packed[:members], experts, pair, width, (0, 1))):
            cols = slice(side * half, (side + 1) * half)
            rows = jnp.concatenate(
                [part for ref in packed[:members] for part in (ref[:, cols], ref[:, width : width + half])], 0
            )
            got = jnp.dot(pick, rows, preferred_element_type=F32).astype(BF)
            for j in range(experts):
                outs[j][:block, cols] = got[j * block : (j + 1) * block]

    def second():
        rows = jnp.concatenate([ref[:, :width].astype(F32)[:pair] for ref in packed[:experts]], 0).astype(BF)
        for k in range(members):
            outs[k][: experts * pair] = rows

    by_core(first, second)


def weigh_body(experts, pair, width, *refs):
    packed, out = refs[:-1], refs[-1]
    tables = tables_of(packed, experts, pair, width, (2, 3, 4))
    out[...] = jnp.concatenate([t.astype(F32).T for t in tables], 0).astype(BF)


def up_body(members, experts, pair, *refs):
    count = (len(refs) - 4) // 2
    mine, theirs, refs = refs[:count], refs[count : 2 * count], refs[2 * count :]
    gate_ref, up_ref, hidden_ref, rows_ref = refs

    def parts(core, blocks):
        number, size = ((experts, members * pair), (members, experts * pair))[core]
        return [b[:size] for b in blocks[:number]]

    def fill(core):
        rows_ref[...] = jnp.concatenate(parts(core, mine) + parts(1 - core, theirs), 0)

    if members == experts:
        fill(0)
    else:
        by_core(lambda: fill(0), lambda: fill(1))
    for j in range(hidden_ref.shape[1] // UNIT_TILE):
        cols = slice(j * UNIT_TILE, (j + 1) * UNIT_TILE)
        gate = jnp.dot(rows_ref[...], gate_ref[:, cols], preferred_element_type=F32)
        up = jnp.dot(rows_ref[...], up_ref[:, cols], preferred_element_type=F32)
        hidden_ref[:, cols] = (jax.nn.silu(gate) * up).astype(BF)


def down_body(first, hidden_ref, down_ref, own_ref, other_ref):
    mine, width = own_ref.shape
    tile = min(512, width)
    for j in range(width // tile):
        cols = slice(j * tile, (j + 1) * tile)
        at = slice(first + j * tile, first + (j + 1) * tile)
        value = jnp.dot(hidden_ref[...], down_ref[:, at], preferred_element_type=F32).astype(BF)
        own_ref[:, cols] = value[:mine]
        other_ref[:, cols] = value[mine:]


def up_down_body(members, experts, pair, *refs):
    ins, (down_ref, hidden_ref, own_ref, other_ref, rows_ref) = refs[:-5], refs[-5:]
    up_body(members, experts, pair, *ins, hidden_ref, rows_ref)
    down_body(0, hidden_ref, down_ref, own_ref, other_ref)


def add_body(members, experts, pair, *refs):
    parts = len(CUTS) - 1
    owns, gots, outs = refs[:parts], refs[parts : 2 * parts], refs[2 * parts :]

    def split(core):
        number, size = ((experts, members * pair), (members, experts * pair))[core]
        for j in range(number):
            at = slice(j * size, (j + 1) * size)
            first = 0
            for own_ref, got_ref in zip(owns, gots):
                cols = slice(first, first + own_ref.shape[1])
                outs[j][:size, cols] = (own_ref[at].astype(F32) + got_ref[at].astype(F32)).astype(BF)
                first += own_ref.shape[1]

    if members == experts:
        split(0)
    else:
        by_core(lambda: split(0), lambda: split(1))


def blend_body(members, experts, pair, weights_ref, *refs):
    count = len(refs) // 2
    values, outs = refs[:count], refs[count:]
    width = values[0].shape[1]
    half = width // 2

    def first():
        tails = []
        for side in range(2):
            cols = slice(side * half, (side + 1) * half)
            value = jnp.concatenate([v[: members * pair, cols] for v in values[:experts]], 0)
            total = weigh_rows(weights_ref[...], value, members * FOLD)
            for k in range(members):
                outs[k][:, cols] = total[k * FOLD : k * FOLD + SUB].astype(BF)
            tails.append([total[k * FOLD + SUB : k * FOLD + SUB + 4] for k in range(members)])
        for k in range(members):
            outs[k][:, width:] = jnp.concatenate([tails[0][k], tails[1][k]], 0).astype(BF)

    def second():
        total = values[0][: experts * pair].astype(F32)
        for v in values[1:members]:
            total = total + v[: experts * pair].astype(F32)
        for j in range(experts):
            outs[j][:, :width] = padded(total[j * pair : (j + 1) * pair]).astype(BF)
            outs[j][:, width:] = jnp.zeros((SUB, half), BF)

    by_core(first, second)


def finish_body(members, experts, pair, table_ref, *refs):
    parts, out_ref = refs[:-1], refs[-1]
    rows, steps, width = out_ref.shape
    half = width // 2

    def write(flat):
        for r in range(rows):
            out_ref[r] = flat[r * steps : (r + 1) * steps].astype(BF)

    def first():
        total = parts[0][...].astype(F32)
        for p in parts[1:members]:
            total = total + p[...].astype(F32)
        tail = total[:, width:]
        tail = jnp.concatenate([tail[:4], tail[4:]], 1)
        write(jnp.concatenate([total[:, :width], tail], 0))

    def second():
        value = jnp.concatenate([p[:, :width].astype(F32)[:pair] for p in parts[:experts]], 0).astype(BF)
        write(weigh_rows(table_ref[:, 2 * FOLD : 5 * FOLD].astype(F32).T.astype(BF), value, FOLD))

    by_core(first, second)


def local(expert_input, expert_ids, combine, gate_weight, up_weight, down_weight):
    members = lax.axis_size("group")
    devices = lax.axis_size("dev")
    experts = devices // 2
    steps, row_count, width = expert_input.shape
    slots = max(2, (2 * row_count + experts - 1) // experts)
    pair = steps * slots
    folded = width + width // 2
    table_rows = experts * pair
    packed_width = folded + table_rows // SUB * LANES
    count = max(members, experts)
    block = count * pair
    rows_half = members * experts * pair
    hidden_units = gate_weight.shape[2]

    offsets = plane_order(experts)

    def send(arrays, group_core, back):
        got = {0: arrays[0]}
        for i in sorted(range(1, count), key=lambda i: -min(i, count - i)):
            pairs = []
            for g in range(members):
                for d in range(devices):
                    if d % 2 == group_core:
                        if i < members:
                            pairs.append((g * devices + d, group_peer(g, i, members, back) * devices + d))
                    elif i < experts:
                        pairs.append((g * devices + d, g * devices + (d ^ (2 * offsets[i]))))
            got[i] = lax.ppermute(arrays[i], ("group", "dev"), pairs)
        return [got[i] for i in range(count)]

    def swap(array):
        return lax.ppermute(array, "dev", [(i, i ^ 1) for i in range(devices)])

    x = expert_input.transpose(1, 0, 2)
    ids = expert_ids.transpose(0, 2, 1)
    scale = combine.transpose(0, 2, 1)
    *packed, table = call(
        functools.partial(pack_body, experts, slots),
        [(SUB, packed_width)] * count + [(table_rows, LANES)],
        [pinned(a) for a in (ids, scale, x)],
        "pack",
        [pltpu.HBM] * 3,
        [
            pltpu.SMEM(ids.shape, ids.dtype),
            pltpu.SMEM(scale.shape, scale.dtype),
            pltpu.VMEM(x.shape, x.dtype),
            pltpu.SemaphoreType.DMA((3,)),
        ],
        flops=BESIDE_TRANSFER,
    )
    arrived = send(packed, 0, False)
    routed = call(
        functools.partial(route_body, members, experts, pair),
        [(block, width)] * count,
        arrived,
        "route",
        flops=BESIDE_TRANSFER,
    )
    mine = send(routed, 1, False)
    theirs = [swap(a) for a in mine]
    (weights,) = call(
        functools.partial(weigh_body, experts, pair, width),
        [(3 * members * FOLD, rows_half)],
        arrived[:members],
        "weigh",
    )
    cuts = [cut * width // CUTS[-1] for cut in CUTS]
    hidden, own, other = call(
        functools.partial(up_down_body, members, experts, pair),
        [(2 * rows_half, hidden_units)] + [(rows_half, cuts[1])] * 2,
        (*mine, *theirs, gate_weight[0], up_weight[0], down_weight[0]),
        "gate_up_down",
        scratch=[pltpu.VMEM((2 * rows_half, width), BF)],
        flops=8 * rows_half * width * hidden_units,
    )
    owns, others = [own], [swap(other)]
    for p, (low, high) in enumerate(zip(cuts[1:], cuts[2:])):
        own, other = call(
            functools.partial(down_body, low),
            [(rows_half, high - low)] * 2,
            (hidden, down_weight[0]),
            "down_%d" % (p + 1),
            flops=4 * rows_half * (high - low) * hidden_units,
        )
        owns.append(own)
        others.append(swap(other))
    halves = call(
        functools.partial(add_body, members, experts, pair), [(block, width)] * count, (*owns, *others), "add"
    )
    returned = send(halves, 1, True)
    blended = call(
        functools.partial(blend_body, members, experts, pair), [(SUB, folded)] * count, (weights, *returned), "blend"
    )
    final = send(blended, 0, True)
    (out,) = call(
        functools.partial(finish_body, members, experts, pair), [(row_count, steps, width)], (table, *final), "finish"
    )
    return out.transpose(1, 0, 2)


def solution(mesh):
    in_specs = (
        P(None, ("group", "dev"), None),
        P(None, ("group", "dev"), None),
        P(None, ("group", "dev"), None),
        P("dev", None, "group"),
        P("dev", None, "group"),
        P("dev", "group", None),
    )
    out_specs = P(None, ("group", "dev"), None)
    return jax.shard_map(local, mesh=mesh, in_specs=in_specs, out_specs=out_specs, check_vma=False)
```

```python
import functools

import jax
import jax.numpy as jnp
from jax import lax
from jax.experimental import pallas as pl
from jax.experimental.pallas import tpu as pltpu
from jax.sharding import PartitionSpec as P

BF = jnp.bfloat16
F32 = jnp.float32
LANES = 128
SUB = 8
FOLD = 16
UNIT_TILE = 256
CUTS = (0, 3, 4)
BESIDE_TRANSFER = 10**10


def group_peer(g, i, members, back):
    ring = [n ^ (n >> 1) for n in range(members)]
    if sorted(ring) != list(range(members)):
        ring = list(range(members))
    return ring[(ring.index(g) + (i if back else -i)) % members]


def plane_order(experts):
    return [0] + sorted(range(1, experts), key=lambda j: (-bin(j).count("1"), j))


def whole(memory_space=pltpu.VMEM):
    return pl.BlockSpec(memory_space=memory_space)


def pinned(array):
    return pltpu.with_memory_space_constraint(array, pltpu.HBM)


def call(body, outs, args, name, spaces=None, scratch=(), limit=12, flops=0):
    spaces = spaces or [pltpu.VMEM] * len(args)
    return pl.pallas_call(
        body,
        out_shape=[jax.ShapeDtypeStruct(s, BF) if isinstance(s, tuple) else s for s in outs],
        in_specs=[whole(s) for s in spaces],
        out_specs=[whole() for _ in outs],
        scratch_shapes=list(scratch),
        name=name,
        compiler_params=pltpu.CompilerParams(vmem_limit_bytes=limit << 20),
        cost_estimate=pl.CostEstimate(flops=flops, bytes_accessed=0, transcendentals=0),
    )(*args)


def by_core(first, second):
    core = lax.axis_index("dev") % 2
    pl.when(core == 0)(first)
    pl.when(core == 1)(second)


def padded(rows):
    missing = -rows.shape[0] % SUB
    return jnp.concatenate([rows, jnp.zeros((missing, rows.shape[1]), rows.dtype)], 0) if missing else rows


def weigh_rows(weights, value, span):
    total = jnp.dot(weights, value, preferred_element_type=F32)
    return total[:span] + total[span : 2 * span] + total[2 * span :]


def pack_body(experts, slots, ids_hbm, combine_hbm, x_hbm, *refs):
    outs, table_out, (ids_ref, combine_ref, x_ref, sems) = refs[:-5], refs[-5], refs[-4:]
    copies = [
        pltpu.make_async_copy(source, target, sems.at[i])
        for i, (source, target) in enumerate(((ids_hbm, ids_ref), (combine_hbm, combine_ref), (x_hbm, x_ref)))
    ]
    for copy in copies:
        copy.start()
    rows, steps, width = x_ref.shape
    half = width // 2
    pair = steps * slots
    own = lax.axis_index("dev") // 2
    offsets = plane_order(experts)
    table_rows = experts * pair
    row_at = lax.broadcasted_iota(jnp.int32, (table_rows, LANES), 0)
    lane = lax.broadcasted_iota(jnp.int32, (table_rows, LANES), 1)
    group, place = lane // FOLD, lane % FOLD
    low = jnp.where((group == 1) & (place >= 12), place - 4, jnp.where((group == 1) & (place >= SUB), -1, place))
    table = jnp.zeros((table_rows, LANES), F32)
    copies[0].wait()
    copies[1].wait()
    turns = sum(offsets.index(offset) << (4 * offset) for offset in range(experts))
    turns = jnp.int32(turns - (1 << 32) if turns >> 31 else turns)
    for t in range(steps):
        counts = jnp.int32(0)
        for r in range(rows):
            for k in range(2):
                e = ids_ref[t, k, r]
                position = (counts >> (4 * e)) & 15
                counts = counts + (1 << (4 * e))
                turn = (turns >> (4 * (e ^ own))) & 15
                slot = (turn * steps + t) * slots + position
                hit = (row_at == slot) & (low == r * steps + t)
                table = jnp.where(hit, combine_ref[t, k, r], table)
    ones = jnp.where(table != 0.0, 1.0, 0.0)
    high = table.astype(BF).astype(F32)
    middle = (table - high).astype(BF).astype(F32)
    rest = table - high - middle
    coded = jnp.where(
        group <= 1, ones, jnp.where(group == 2, high, jnp.where(group == 3, middle, jnp.where(group == 4, rest, 0.0)))
    ).astype(BF)
    table_out[...] = coded
    copies[2].wait()
    flat = jnp.concatenate([x_ref[r].astype(F32) for r in range(rows)], 0)

    def first():
        tail = flat[SUB:]
        top = flat[:SUB].astype(BF)
        fold = jnp.concatenate([tail[:, :half], tail[:, half:]], 0).astype(BF)
        for out in outs:
            out[:, :width] = top
            out[:, width : width + half] = fold
            for b in range(table_rows // SUB):
                start = width + half + b * LANES
                out[:, start : start + LANES] = coded[b * SUB : (b + 1) * SUB]

    def second():
        source = jnp.concatenate([flat, jnp.zeros((FOLD - flat.shape[0], width), F32)], 0).astype(BF)
        got = jnp.dot(coded[:, :FOLD], source, preferred_element_type=F32)
        for j, out in enumerate(outs):
            if j < experts:
                out[:, :width] = padded(got[j * pair : (j + 1) * pair]).astype(BF)
            else:
                out[:, :width] = jnp.zeros((SUB, width), BF)
            out[:, width:] = jnp.zeros((SUB, out.shape[1] - width), BF)

    by_core(first, second)


def tables_of(packed, experts, pair, width, groups):
    base = width + width // 2
    members = len(packed)
    table_rows = experts * pair
    total = table_rows * members
    span = -(-members * FOLD // LANES) * LANES
    blocks = []
    for k, ref in enumerate(packed):
        tab = jnp.concatenate(
            [ref[:, base + b * LANES : base + (b + 1) * LANES] for b in range(table_rows // SUB)], 0
        ).astype(F32)
        at = k % (LANES // FOLD)
        here = lax.broadcasted_iota(jnp.int32, tab.shape, 1) // FOLD == at
        tiles = []
        for group in groups:
            shift = (at - group) * FOLD % LANES
            moved = jnp.where(here, pltpu.roll(tab, shift, 1) if shift else tab, 0.0)
            row = [jnp.zeros_like(moved)] * (span // LANES)
            row[k * FOLD // LANES] = moved
            tiles += row
        blocks.append(jnp.concatenate(tiles, 1))
    stacked = jnp.concatenate(blocks, 0).astype(BF)
    to = lax.broadcasted_iota(jnp.int32, (total, total), 0)
    source = lax.broadcasted_iota(jnp.int32, (total, total), 1)
    e, k, p = to // (members * pair), to // pair % members, to % pair
    order = jnp.where(source == k * table_rows + e * pair + p, 1.0, 0.0).astype(BF)
    all_groups = jnp.dot(order, stacked, preferred_element_type=F32).astype(BF)
    return [all_groups[:, i * span : i * span + members * FOLD] for i in range(len(groups))]


def route_body(members, experts, pair, *refs):
    count = len(refs) // 2
    packed, outs = refs[:count], refs[count:]
    width = outs[0].shape[1]
    half = width // 2

    def first():
        block = members * pair
        for side, pick in enumerate(tables_of(packed[:members], experts, pair, width, (0, 1))):
            cols = slice(side * half, (side + 1) * half)
            rows = jnp.concatenate(
                [part for ref in packed[:members] for part in (ref[:, cols], ref[:, width : width + half])], 0
            )
            got = jnp.dot(pick, rows, preferred_element_type=F32).astype(BF)
            for j in range(experts):
                outs[j][:block, cols] = got[j * block : (j + 1) * block]

    def second():
        rows = jnp.concatenate([ref[:, :width].astype(F32)[:pair] for ref in packed[:experts]], 0).astype(BF)
        for k in range(members):
            outs[k][: experts * pair] = rows

    by_core(first, second)


def weigh_body(experts, pair, width, *refs):
    packed, out = refs[:-1], refs[-1]
    tables = tables_of(packed, experts, pair, width, (2, 3, 4))
    out[...] = jnp.concatenate([t.astype(F32).T for t in tables], 0).astype(BF)


def up_body(members, experts, pair, *refs):
    count = (len(refs) - 4) // 2
    mine, theirs, refs = refs[:count], refs[count : 2 * count], refs[2 * count :]
    gate_ref, up_ref, hidden_ref, rows_ref = refs

    def parts(core, blocks):
        number, size = ((experts, members * pair), (members, experts * pair))[core]
        return [b[:size] for b in blocks[:number]]

    def fill(core):
        rows_ref[...] = jnp.concatenate(parts(core, mine) + parts(1 - core, theirs), 0)

    if members == experts:
        fill(0)
    else:
        by_core(lambda: fill(0), lambda: fill(1))
    tile = UNIT_TILE * (2 if rows_ref.shape[0] <= UNIT_TILE else 1)
    for j in range(hidden_ref.shape[1] // tile):
        cols = slice(j * tile, (j + 1) * tile)
        gate = jnp.dot(rows_ref[...], gate_ref[:, cols], preferred_element_type=F32)
        up = jnp.dot(rows_ref[...], up_ref[:, cols], preferred_element_type=F32)
        hidden_ref[:, cols] = (jax.nn.silu(gate) * up).astype(BF)


def down_body(first, hidden_ref, down_ref, own_ref, other_ref):
    mine, width = own_ref.shape
    tile = min(512, width)
    for j in range(width // tile):
        cols = slice(j * tile, (j + 1) * tile)
        at = slice(first + j * tile, first + (j + 1) * tile)
        value = jnp.dot(hidden_ref[...], down_ref[:, at], preferred_element_type=F32).astype(BF)
        own_ref[:, cols] = value[:mine]
        other_ref[:, cols] = value[mine:]


def up_down_body(members, experts, pair, *refs):
    ins, (down_ref, hidden_ref, own_ref, other_ref, rows_ref) = refs[:-5], refs[-5:]
    up_body(members, experts, pair, *ins, hidden_ref, rows_ref)
    down_body(0, hidden_ref, down_ref, own_ref, other_ref)


def add_body(members, experts, pair, *refs):
    parts = len(CUTS) - 1
    owns, gots, outs = refs[:parts], refs[parts : 2 * parts], refs[2 * parts :]

    def split(core):
        number, size = ((experts, members * pair), (members, experts * pair))[core]
        for j in range(number):
            at = slice(j * size, (j + 1) * size)
            first = 0
            for own_ref, got_ref in zip(owns, gots):
                cols = slice(first, first + own_ref.shape[1])
                outs[j][:size, cols] = (own_ref[at].astype(F32) + got_ref[at].astype(F32)).astype(BF)
                first += own_ref.shape[1]

    if members == experts:
        split(0)
    else:
        by_core(lambda: split(0), lambda: split(1))


def blend_body(members, experts, pair, weights_ref, *refs):
    count = len(refs) // 2
    values, outs = refs[:count], refs[count:]
    width = values[0].shape[1]
    half = width // 2

    def first():
        tails = []
        for side in range(2):
            cols = slice(side * half, (side + 1) * half)
            value = jnp.concatenate([v[: members * pair, cols] for v in values[:experts]], 0)
            total = weigh_rows(weights_ref[...], value, members * FOLD)
            for k in range(members):
                outs[k][:, cols] = total[k * FOLD : k * FOLD + SUB].astype(BF)
            tails.append([total[k * FOLD + SUB : k * FOLD + SUB + 4] for k in range(members)])
        for k in range(members):
            outs[k][:, width:] = jnp.concatenate([tails[0][k], tails[1][k]], 0).astype(BF)

    def second():
        total = values[0][: experts * pair].astype(F32)
        for v in values[1:members]:
            total = total + v[: experts * pair].astype(F32)
        for j in range(experts):
            outs[j][:, :width] = padded(total[j * pair : (j + 1) * pair]).astype(BF)
            outs[j][:, width:] = jnp.zeros((SUB, half), BF)

    by_core(first, second)


def finish_body(members, experts, pair, table_ref, *refs):
    parts, out_ref = refs[:-1], refs[-1]
    rows, steps, width = out_ref.shape
    half = width // 2

    def write(flat):
        for r in range(rows):
            out_ref[r] = flat[r * steps : (r + 1) * steps].astype(BF)

    def first():
        total = parts[0][...].astype(F32)
        for p in parts[1:members]:
            total = total + p[...].astype(F32)
        tail = total[:, width:]
        tail = jnp.concatenate([tail[:4], tail[4:]], 1)
        write(jnp.concatenate([total[:, :width], tail], 0))

    def second():
        value = jnp.concatenate([p[:, :width].astype(F32)[:pair] for p in parts[:experts]], 0).astype(BF)
        write(weigh_rows(table_ref[:, 2 * FOLD : 5 * FOLD].astype(F32).T.astype(BF), value, FOLD))

    by_core(first, second)


def local(expert_input, expert_ids, combine, gate_weight, up_weight, down_weight):
    members = lax.axis_size("group")
    devices = lax.axis_size("dev")
    experts = devices // 2
    steps, row_count, width = expert_input.shape
    slots = max(2, (2 * row_count + experts - 1) // experts)
    pair = steps * slots
    folded = width + width // 2
    table_rows = experts * pair
    packed_width = folded + table_rows // SUB * LANES
    count = max(members, experts)
    block = count * pair
    rows_half = members * experts * pair
    hidden_units = gate_weight.shape[2]

    offsets = plane_order(experts)

    def send(arrays, group_core, back):
        got = {0: arrays[0]}
        for i in sorted(range(1, count), key=lambda i: -min(i, count - i)):
            pairs = []
            for g in range(members):
                for d in range(devices):
                    if d % 2 == group_core:
                        if i < members:
                            pairs.append((g * devices + d, group_peer(g, i, members, back) * devices + d))
                    elif i < experts:
                        pairs.append((g * devices + d, g * devices + (d ^ (2 * offsets[i]))))
            got[i] = lax.ppermute(arrays[i], ("group", "dev"), pairs)
        return [got[i] for i in range(count)]

    def swap(array):
        return lax.ppermute(array, "dev", [(i, i ^ 1) for i in range(devices)])

    x = expert_input.transpose(1, 0, 2)
    ids = expert_ids.transpose(0, 2, 1)
    scale = combine.transpose(0, 2, 1)
    *packed, table = call(
        functools.partial(pack_body, experts, slots),
        [(SUB, packed_width)] * count + [(table_rows, LANES)],
        [pinned(a) for a in (ids, scale, x)],
        "pack",
        [pltpu.HBM] * 3,
        [
            pltpu.SMEM(ids.shape, ids.dtype),
            pltpu.SMEM(scale.shape, scale.dtype),
            pltpu.VMEM(x.shape, x.dtype),
            pltpu.SemaphoreType.DMA((3,)),
        ],
        flops=BESIDE_TRANSFER,
    )
    arrived = send(packed, 0, False)
    routed = call(
        functools.partial(route_body, members, experts, pair),
        [(block, width)] * count,
        arrived,
        "route",
        flops=BESIDE_TRANSFER,
    )
    mine = send(routed, 1, False)
    theirs = [swap(a) for a in mine]
    (weights,) = call(
        functools.partial(weigh_body, experts, pair, width),
        [(3 * members * FOLD, rows_half)],
        arrived[:members],
        "weigh",
    )
    cuts = [cut * width // CUTS[-1] for cut in CUTS]
    hidden, own, other = call(
        functools.partial(up_down_body, members, experts, pair),
        [(2 * rows_half, hidden_units)] + [(rows_half, cuts[1])] * 2,
        (*mine, *theirs, gate_weight[0], up_weight[0], down_weight[0]),
        "gate_up_down",
        scratch=[pltpu.VMEM((2 * rows_half, width), BF)],
        flops=8 * rows_half * width * hidden_units,
    )
    owns, others = [own], [swap(other)]
    for p, (low, high) in enumerate(zip(cuts[1:], cuts[2:])):
        own, other = call(
            functools.partial(down_body, low),
            [(rows_half, high - low)] * 2,
            (hidden, down_weight[0]),
            "down_%d" % (p + 1),
            flops=4 * rows_half * (high - low) * hidden_units,
        )
        owns.append(own)
        others.append(swap(other))
    halves = call(
        functools.partial(add_body, members, experts, pair), [(block, width)] * count, (*owns, *others), "add"
    )
    returned = send(halves, 1, True)
    blended = call(
        functools.partial(blend_body, members, experts, pair), [(SUB, folded)] * count, (weights, *returned), "blend"
    )
    final = send(blended, 0, True)
    (out,) = call(
        functools.partial(finish_body, members, experts, pair), [(row_count, steps, width)], (table, *final), "finish"
    )
    return out.transpose(1, 0, 2)


def solution(mesh):
    in_specs = (
        P(None, ("group", "dev"), None),
        P(None, ("group", "dev"), None),
        P(None, ("group", "dev"), None),
        P("dev", None, "group"),
        P("dev", None, "group"),
        P("dev", "group", None),
    )
    out_specs = P(None, ("group", "dev"), None)
    return jax.shard_map(local, mesh=mesh, in_specs=in_specs, out_specs=out_specs, check_vma=False)
```
